32 devices in a mesh: seq: 8 (over z, y), head: 4 (over x, core).
Axes of the slice: x: 2, y: 2, z: 4, core: 2. Of those that a mesh axis runs over, the one named last changes fastest.
Arguments:
- query_rows: bfloat16 [1024, 512], P('seq', 'head'), may hold values from -6 to 6
- key_rows: bfloat16 [1024, 512], P('seq', 'head'), may hold values from -6 to 6
- value_rows: bfloat16 [1024, 512], P('seq', 'head'), may hold values from -6 to 6
- gate_rows: bfloat16 [1024, 512], P('seq', 'head'), may hold values from -6 to 6
- cotangent: bfloat16 [1024, 512], P('seq', 'head'), may hold values from -6 to 6
- event_gaps: int32 [1024], P('seq'), may hold values from 0 to 7
- block_lists: int32 [8, 8], replicated, may hold values from -1 to 6, as said below
- bias_table: float32 [8, 16], P('head'), may hold values from -1 to 1
- norm_gain: float32 [512], P('head'), may hold values from 0.1 to 1.9
Outputs:
- layer_out: bfloat16 [1024, 512], P('seq', 'head')
- grad_query: bfloat16 [1024, 512], P('seq', 'head')
- grad_key: bfloat16 [1024, 512], P('seq', 'head')
- grad_value: bfloat16 [1024, 512], P('seq', 'head')
- grad_gate: bfloat16 [1024, 512], P('seq', 'head')
The draws below stay inside these ranges and needn't reach their ends.
Inputs may be any that keep to these rules, and one draw needn't show every extreme that they name: `block_lists`: slot s of row c holds either c - 2**s or -1; it holds -1 wherever 2**s >= 8 or 2**s > c. The last row lists every group c - 2**s that exists.
All inputs are finite; a program needn't handle non-finite values.
Results may differ from the reference program's by a relative error of at most 0.01.
Values may be sent and summed in bfloat16 or wider, within the bound.
A program may use at most 64 MiB of HBM per device.

```python
import jax
import jax.numpy as jnp
from jax import lax

H = 8
DH = 64
D = 512
C = 128
NB = 8
NBK = 16
NCH = 8
L = 1024


def draw_block_lists(key, part):
    group_ids = jnp.arange(NCH, dtype=jnp.int32)[:, None]
    slot_ids = jnp.arange(NB, dtype=jnp.int32)[None, :]
    distance = jnp.left_shift(jnp.int32(1), slot_ids)
    density = jax.random.randint(jax.random.fold_in(key, 11), (NCH, 1), 1, 5)
    coins = jax.random.randint(jax.random.fold_in(key, 12), (NCH, NB), 0, 4)
    exists = (distance < NCH) & (group_ids - distance >= 0)
    chosen = (coins < density) | (group_ids == NCH - 1)
    return jnp.where(exists & chosen, group_ids - distance, -1).astype(jnp.int32)


def plant(entries, rng, least, high):
    dims = entries.shape
    place = [jax.random.randint(jax.random.fold_in(rng, axis), (), 0, dims[axis]) for axis in range(len(dims))]
    entries = entries.at[tuple(place)].set(least)
    longest = dims.index(max(dims))
    place[longest] = (place[longest] + 1) % dims[longest]
    return entries.at[tuple(place)].set(high)


def level_of(own_key, extent, pieces, low, largest):
    def one(dim, shards_of):
        heights = jax.random.uniform(jax.random.fold_in(jax.random.fold_in(own_key, 6), dim), (shards_of,), jnp.float32, low / len(pieces), largest / len(pieces))
        return jnp.repeat(jnp.exp(heights), extent[dim] // shards_of).reshape((-1,) + (1,) * (len(extent) - dim - 1))

    loudness = one(*pieces[0])
    for cut in pieces[1:]:
        loudness = loudness * one(*cut)
    return loudness


def bell_draw(stream_key, extent, spread, most, pieces=(), kind=jnp.bfloat16):
    level = level_of(stream_key, extent, pieces, -0.22, 0.18) if pieces else 1.0
    values = jax.random.normal(stream_key, extent, jnp.float32) * spread * level
    return jnp.minimum(jnp.maximum(values, -most), most).astype(kind)


def setup_inputs(seed: int = 0) -> dict:
    splits = jax.random.split(jax.random.key(seed), 10)
    return {
        "query_rows": bell_draw(splits[0], (L, D), 1.0, 6.0, ((0, 8), (1, 4))),
        "key_rows": bell_draw(splits[1], (L, D), 1.0, 6.0, ((0, 8), (1, 4))),
        "value_rows": bell_draw(splits[2], (L, D), 1.0, 6.0, ((0, 8), (1, 4))),
        "gate_rows": bell_draw(splits[3], (L, D), 1.0, 6.0, ((0, 8), (1, 4))),
        "cotangent": bell_draw(splits[4], (L, D), 1.0, 6.0, ((0, 8), (1, 4))),
        "event_gaps": plant(jax.random.randint(splits[5], (L,), 0, 8), jax.random.fold_in(splits[5], 1), 0, 7).astype(jnp.int32),
        "block_lists": draw_block_lists(jax.random.fold_in(splits[9], 71), 0),
        "bias_table": jnp.clip(jax.random.uniform(splits[7], (H, NBK), jnp.float32, -1.0, 1.0) * level_of(splits[7], (H, NBK), ((0, 4),), -0.4, 0.0), -1.0, 1.0),
        "norm_gain": jnp.clip(1.0 + 0.18 * jax.random.normal(splits[8], (D,), jnp.float32), 0.1, 1.9),
    }


norm_eps = 1e-05

def bucket_bias(delta, table):
    bias = jnp.zeros((table.shape[0],) + delta.shape, jnp.float32) + table[:, 0][:, None, None]
    for bucket_id in range(1, table.shape[1]):
        increment = (table[:, bucket_id] - table[:, bucket_id - 1])[:, None, None]
        reached = (delta >= 2 ** (bucket_id - 1)).astype(jnp.float32)
        bias = bias + increment * reached[None]
    return bias

def causal_mask(length):
    later_ids = lax.broadcasted_iota(jnp.int32, (length, length), 1)
    early_ids = lax.broadcasted_iota(jnp.int32, (length, length), 0)
    return (later_ids <= early_ids).astype(jnp.float32)

def block_scores(query_heads, key_heads, query_times, key_times, table, scaling):
    scores = jnp.einsum('qhd,khd->hqk', query_heads.astype(jnp.float32), key_heads.astype(jnp.float32)) * scaling
    return scores + bucket_bias(query_times[:, None] - key_times[None, :], table)

def pick_group(array, index):
    return lax.dynamic_index_in_dim(array, index, 0, keepdims=False)

def reference(query_rows, key_rows, value_rows, gate_rows, cotangent, event_gaps, block_lists, bias_table, norm_gain):
    scaling = DH ** (-0.5)
    event_times = jnp.cumsum(event_gaps).astype(jnp.int32)
    query_all = query_rows.reshape(NCH, C, H, DH)
    key_all = key_rows.reshape(NCH, C, H, DH)
    value_all = value_rows.reshape(NCH, C, H, DH)
    gate_all = gate_rows.reshape(NCH, C, D)
    upstream_all = cotangent.reshape(NCH, C, D)
    times_all = event_times.reshape(NCH, C)
    diagonal = causal_mask(C)
    offsets = [(slot_id, 2 ** slot_id) for slot_id in range(NB) if 2 ** slot_id < NCH]

    def one_group(accum, group_id):
        key_grad, value_grad = accum
        query_heads = pick_group(query_all, group_id)
        query_times = pick_group(times_all, group_id)
        sources = [(group_id, group_id >= 0, True)]
        for slot_id, distance in offsets:
            sources.append((jnp.maximum(group_id - distance, 0), block_lists[group_id, slot_id] >= 0, False))
        attended = jnp.zeros((C, H, DH), jnp.float32)
        for source, listed, on_diag in sources:
            key_heads = pick_group(key_all, source)
            value_heads = pick_group(value_all, source)
            scores = block_scores(query_heads, key_heads, query_times, pick_group(times_all, source), bias_table, scaling)
            weights = jax.nn.silu(scores)
            if on_diag:
                weights = weights * diagonal[None]
            weights = weights.astype(jnp.bfloat16)
            added = jnp.einsum('hqk,khd->qhd', weights.astype(jnp.float32), value_heads.astype(jnp.float32))
            attended = attended + jnp.where(listed, added, 0.0)
        flat = attended.reshape(C, D)
        row_mean = lax.optimization_barrier(jnp.sum(flat, axis=1)) / D
        row_var = lax.optimization_barrier(jnp.sum(flat * flat, axis=1)) / D - row_mean * row_mean
        inv_std = lax.rsqrt(row_var + norm_eps)
        centered = (flat - row_mean[:, None]) * inv_std[:, None]
        normed = centered * norm_gain[None, :]
        gates = pick_group(gate_all, group_id).astype(jnp.float32)
        upstream = pick_group(upstream_all, group_id).astype(jnp.float32)
        layer_out = (normed * gates).astype(jnp.bfloat16)
        grad_gate = (upstream * normed).astype(jnp.bfloat16)
        scaled = upstream * gates * norm_gain[None, :]
        grad_attended = inv_std[:, None] * (scaled - lax.optimization_barrier(jnp.sum(scaled, axis=1))[:, None] / D - centered * lax.optimization_barrier(jnp.sum(scaled * centered, axis=1))[:, None] / D)
        grad_heads = grad_attended.astype(jnp.bfloat16).reshape(C, H, DH)
        grad_query = jnp.zeros((C, H, DH), jnp.float32)
        for source, listed, on_diag in sources:
            key_heads = pick_group(key_all, source)
            value_heads = pick_group(value_all, source)
            scores = block_scores(query_heads, key_heads, query_times, pick_group(times_all, source), bias_table, scaling)
            sigmoid_val = jax.nn.sigmoid(scores)
            weights = jax.nn.silu(scores)
            slope = sigmoid_val * (1.0 + scores * (1.0 - sigmoid_val))
            grad_weights = jnp.einsum('qhd,khd->hqk', grad_heads.astype(jnp.float32), value_heads.astype(jnp.float32))
            grad_scores = grad_weights * slope
            if on_diag:
                weights = weights * diagonal[None]
                grad_scores = grad_scores * diagonal[None]
            weights = weights.astype(jnp.bfloat16).astype(jnp.float32)
            grad_scores = grad_scores.astype(jnp.bfloat16).astype(jnp.float32)
            query_part = jnp.einsum('hqk,khd->qhd', grad_scores, key_heads.astype(jnp.float32)) * scaling
            key_part = jnp.einsum('hqk,qhd->khd', grad_scores, query_heads.astype(jnp.float32)) * scaling
            value_part = jnp.einsum('hqk,qhd->khd', weights, grad_heads.astype(jnp.float32))
            grad_query = grad_query + jnp.where(listed, query_part, 0.0)
            key_grad = key_grad.at[source].add(jnp.where(listed, key_part, 0.0))
            value_grad = value_grad.at[source].add(jnp.where(listed, value_part, 0.0))
        return ((key_grad, value_grad), (layer_out, grad_query.reshape(C, D).astype(jnp.bfloat16), grad_gate))
    start = (jnp.zeros((NCH, C, H, DH), jnp.float32), jnp.zeros((NCH, C, H, DH), jnp.float32))
    finals, stacked = lax.scan(one_group, start, jnp.arange(NCH, dtype=jnp.int32))
    layer_out = stacked[0].reshape(L, D)
    grad_query = stacked[1].reshape(L, D)
    grad_gate = stacked[2].reshape(L, D)
    grad_key = finals[0].reshape(L, D).astype(jnp.bfloat16)
    grad_value = finals[1].reshape(L, D).astype(jnp.bfloat16)
    return (layer_out, grad_query, grad_key, grad_value, grad_gate)
```

```python
import functools

import jax
import jax.numpy as jnp
from jax import lax
from jax.experimental import pallas as pl
from jax.experimental.pallas import tpu as pltpu
from jax.sharding import PartitionSpec as P

norm_eps = 1e-05
f32 = jnp.float32
bf16 = jnp.bfloat16
MESH = pl.DeviceIdType.MESH


def mm(a, b):
    return lax.dot_general(a, b, (((1,), (0,)), ((), ())), preferred_element_type=f32)


def mm_nt(a, b):
    return lax.dot_general(a, b, (((1,), (1,)), ((), ())), preferred_element_type=f32)


def kernel(
    groups,
    head_devices,
    offsets,
    q_in,
    k_in,
    v_in,
    gate_ref,
    cot_ref,
    gaps_ref,
    lists_ref,
    table_ref,
    gain_ref,
    layer_ref,
    dq_ref,
    dk_ref,
    dv_ref,
    dgate_ref,
    qbuf,
    kbuf,
    vbuf,
    gabuf,
    gprev,
    glater,
    sums_out,
    sums_in,
    slope_q,
    slope_k,
    weight_k,
    local_sem,
    gap_send,
    gap_recv,
    q_send,
    q_recv,
    kv_send,
    kv_recv,
    sum_send,
    sum_recv,
    ga_send,
    ga_recv,
):
    rows, feats = q_in.shape
    heads, buckets = table_ref.shape
    head_dim = feats // heads
    scaling = head_dim**-0.5
    full_width = feats * head_devices
    reach = offsets[-1]
    count = len(offsets)
    me = lax.axis_index("seq")
    head = lax.axis_index("head")

    def to_later(d, body):
        pl.when(me + d < groups)(body)

    def to_earlier(d, body):
        pl.when(me >= d)(body)

    barrier = pltpu.get_barrier_semaphore()

    def greet(axis, where):
        pl.semaphore_signal(barrier, inc=1, device_id={axis: where}, device_id_type=MESH)

    for k in range(1, reach + 1):
        to_later(k, lambda k=k: greet("seq", me + k))
        to_earlier(k, lambda k=k: greet("seq", me - k))
    for r in range(1, head_devices):
        greet("head", lax.rem(head + r, head_devices))
    own = [
        pltpu.make_async_copy(src, dst.at[0], local_sem.at[i])
        for i, (src, dst) in enumerate(((q_in, qbuf), (k_in, kbuf), (v_in, vbuf)))
    ]
    for copy in own:
        copy.start()
    pl.semaphore_wait(
        barrier,
        jnp.minimum(me, reach) + jnp.minimum(groups - 1 - me, reach) + head_devices - 1,
    )

    def remote(src, dst, send, recv, axis, where):
        return pltpu.make_async_remote_copy(
            src_ref=src,
            dst_ref=dst,
            send_sem=send,
            recv_sem=recv,
            device_id={axis: where},
            device_id_type=MESH,
        )

    def gaps_up(k):
        return remote(
            gaps_ref, gprev.at[k - 1], gap_send.at[0, k - 1], gap_recv.at[0, k - 1], "seq", me + k
        )

    def gaps_down(k):
        return remote(
            gaps_ref, glater.at[k - 1], gap_send.at[1, k - 1], gap_recv.at[1, k - 1], "seq", me - k
        )

    def keys_up(s):
        return remote(
            k_in, kbuf.at[s + 1], kv_send.at[0, s], kv_recv.at[0, s], "seq", me + offsets[s]
        )

    def values_up(s):
        return remote(
            v_in, vbuf.at[s + 1], kv_send.at[1, s], kv_recv.at[1, s], "seq", me + offsets[s]
        )

    def queries_down(s):
        return remote(q_in, qbuf.at[s + 1], q_send.at[s], q_recv.at[s], "seq", me - offsets[s])

    def grads_down(s):
        return remote(
            gabuf.at[0], gabuf.at[s + 1], ga_send.at[s], ga_recv.at[s], "seq", me - offsets[s]
        )

    def sums_to(r):
        return remote(
            sums_out,
            sums_in.at[r - 1],
            sum_send.at[r - 1],
            sum_recv.at[r - 1],
            "head",
            lax.rem(head + r, head_devices),
        )

    for k in range(1, reach + 1):
        to_later(k, lambda k=k: gaps_up(k).start())
        to_earlier(k, lambda k=k: gaps_down(k).start())
    for s in reversed(range(count)):
        to_later(offsets[s], lambda s=s: keys_up(s).start())
        to_later(offsets[s], lambda s=s: values_up(s).start())
        to_earlier(offsets[s], lambda s=s: queries_down(s).start())

    for k in range(1, reach + 1):

        def no_earlier(k=k):
            gprev[k - 1] = jnp.zeros_like(gprev[k - 1])

        def no_later(k=k):
            glater[k - 1] = jnp.zeros_like(glater[k - 1])

        pl.when(me < k)(no_earlier)
        pl.when(me + k >= groups)(no_later)
    for s, d in enumerate(offsets):

        def no_keys(s=s):
            kbuf[s + 1] = jnp.zeros((rows, feats), bf16)
            vbuf[s + 1] = jnp.zeros((rows, feats), bf16)

        def no_queries(s=s):
            qbuf[s + 1] = jnp.zeros((rows, feats), bf16)
            gabuf[s + 1] = jnp.zeros((feats, rows), bf16)

        pl.when(me < d)(no_keys)
        pl.when(me + d >= groups)(no_queries)

    row_ids = lax.broadcasted_iota(jnp.int32, (rows, rows), 0)
    col_ids = lax.broadcasted_iota(jnp.int32, (rows, rows), 1)
    upper = (row_ids <= col_ids).astype(f32)
    upper_bf = upper.astype(bf16)
    ones = jnp.ones((rows, rows), bf16)
    lane_head = lax.broadcasted_iota(jnp.int32, (rows, feats), 1) // head_dim
    sub_head = lax.broadcasted_iota(jnp.int32, (feats, rows), 0) // head_dim
    lane_masks = [(lane_head == h).astype(bf16) for h in range(heads)]
    sub_masks = [(sub_head == h).astype(bf16) for h in range(heads)]

    def prefix_row(gaps):
        wide = jnp.broadcast_to(gaps, (8, rows)).astype(bf16)
        return mm(wide, upper_bf)[0:1]

    def after_column(gaps):
        return mm(jnp.where(col_ids > row_ids, gaps, 0.0).astype(bf16), ones)

    def bias(delta):
        parts = [jnp.full(delta.shape, table_ref[h, 0], f32) for h in range(heads)]
        for b in range(1, buckets):
            reached = delta >= float(2 ** (b - 1))
            parts = [jnp.where(reached, table_ref[h, b], parts[h]) for h in range(heads)]
        return jnp.concatenate(parts, axis=1)

    def by_head_rows(q):
        return jnp.concatenate([q * mask for mask in lane_masks], axis=0)

    def by_head_lanes(g):
        return jnp.concatenate([g * mask for mask in sub_masks], axis=1)

    def own_heads(wide):
        return jnp.concatenate(
            [
                wide[h * head_dim : (h + 1) * head_dim, h * rows : (h + 1) * rows]
                for h in range(heads)
            ],
            axis=0,
        )

    def activate(keys, queries, biases, mask):
        scores = mm_nt(keys, queries) * scaling + biases
        sig = 0.5 * jnp.tanh(0.5 * scores) + 0.5
        weights = scores * sig
        slope = sig + weights * (1.0 - sig)
        return (weights * mask).astype(bf16), slope * mask

    own_gaps = gaps_ref[...].astype(f32)
    own_total = jnp.sum(own_gaps, axis=1, keepdims=True)
    own_row = prefix_row(own_gaps)
    own_after = after_column(own_gaps)
    diag_bias = bias(own_row + own_after - own_total)
    diag_mask = jnp.concatenate([upper] * heads, axis=1)
    gain = gain_ref[...]
    gates = gate_ref[...].astype(f32)
    upstream = cot_ref[...].astype(f32)
    scaled = (upstream * gates * gain).T

    for copy in own:
        copy.wait()
    keys = kbuf[0]
    values = vbuf[0]
    queries = by_head_rows(qbuf[0])
    diag_weights, diag_slope = activate(keys, queries, diag_bias, diag_mask)
    attended = mm(values.T, diag_weights)

    for k in range(1, reach + 1):
        to_earlier(k, lambda k=k: gaps_up(k).wait_recv())
        to_later(k, lambda k=k: gaps_down(k).wait_recv())

    def between(buf, d):
        if d == 1:
            return jnp.zeros((1, 1), f32)
        return jnp.sum(
            jnp.sum(buf[0 : d - 1].astype(f32), axis=0), axis=1, keepdims=True
        )

    biases = []
    for s, d in enumerate(offsets):
        after = after_column(gprev[d - 1].astype(f32))
        biases.append(bias(own_row + after + between(gprev, d)))
    for s in reversed(range(count)):
        d = offsets[s]
        to_earlier(d, lambda s=s: keys_up(s).wait_recv())
        to_earlier(d, lambda s=s: values_up(s).wait_recv())
    for s in range(count):
        listed = (lists_ref[me, s] >= 0).astype(f32)
        weights, slope = activate(kbuf[s + 1], queries, biases[s], listed)
        slope_q[s] = slope
        attended = attended + mm(vbuf[s + 1].T, weights)

    flat = own_heads(attended)
    own_sums = [
        jnp.sum(x, axis=0, keepdims=True) for x in (flat, flat * flat, scaled, scaled * flat)
    ]
    sums_out[...] = jnp.concatenate(own_sums + [jnp.zeros((4, rows), f32)], axis=0)
    for r in range(1, head_devices):
        sums_to(r).start()

    for s in reversed(range(count)):
        to_later(offsets[s], lambda s=s: queries_down(s).wait_recv())
    for s, d in enumerate(offsets):
        row = prefix_row(glater[d - 1].astype(f32))
        later_bias = bias(row + own_after + between(glater, d))
        there = jnp.minimum(me + d, groups - 1)
        listed = ((lists_ref[there, s] >= 0) & (me + d < groups)).astype(f32)
        weights, slope = activate(keys, by_head_rows(qbuf[s + 1]), later_bias, listed)
        weight_k[s] = weights
        slope_k[s] = slope

    for r in range(1, head_devices):
        sums_to(r).wait_recv()
    sums = sums_out[...]
    for r in range(1, head_devices):
        sums = sums + sums_in[r - 1]
    mean = sums[0:1] / full_width
    var = sums[1:2] / full_width - mean * mean
    inv_std = lax.rsqrt(var + norm_eps)
    centered = (flat - mean) * inv_std
    scaled_mean = sums[2:3] / full_width
    product_mean = inv_std * (sums[3:4] - mean * sums[2:3]) / full_width
    grad = (inv_std * (scaled - scaled_mean - centered * product_mean)).astype(bf16)
    gabuf[0] = grad
    for s in reversed(range(count)):
        to_earlier(offsets[s], lambda s=s: grads_down(s).start())

    grads = by_head_lanes(grad)
    diag_grad = (mm(values, grads) * diag_slope).astype(bf16)
    dq = mm(keys.T, diag_grad)
    dk = mm(diag_grad, queries)
    dv = mm_nt(diag_weights, grads)
    for s in range(count):
        grad_scores = (mm(vbuf[s + 1], grads) * slope_q[s]).astype(bf16)
        dq = dq + mm(kbuf[s + 1].T, grad_scores)
    dq_ref[...] = (own_heads(dq) * scaling).T.astype(bf16)
    normed = centered.T * gain
    layer_ref[...] = (normed * gates).astype(bf16)
    dgate_ref[...] = (upstream * normed).astype(bf16)

    for s in reversed(range(count)):
        to_later(offsets[s], lambda s=s: grads_down(s).wait_recv())
    for s in range(count):
        grads = by_head_lanes(gabuf[s + 1])
        grad_scores = (mm(values, grads) * slope_k[s]).astype(bf16)
        dk = dk + mm(grad_scores, by_head_rows(qbuf[s + 1]))
        dv = dv + mm_nt(weight_k[s], grads)
    dk_ref[...] = (dk * scaling).astype(bf16)
    dv_ref[...] = dv.astype(bf16)

    for k in range(1, reach + 1):
        to_later(k, lambda k=k: gaps_up(k).wait_send())
        to_earlier(k, lambda k=k: gaps_down(k).wait_send())
    for s, d in enumerate(offsets):
        to_later(d, lambda s=s: keys_up(s).wait_send())
        to_later(d, lambda s=s: values_up(s).wait_send())
        to_earlier(d, lambda s=s: queries_down(s).wait_send())
        to_earlier(d, lambda s=s: grads_down(s).wait_send())
    for r in range(1, head_devices):
        sums_to(r).wait_send()


def per_device(
    query_rows,
    key_rows,
    value_rows,
    gate_rows,
    cotangent,
    event_gaps,
    block_lists,
    bias_table,
    norm_gain,
):
    rows, feats = query_rows.shape
    heads = bias_table.shape[0]
    groups = lax.axis_size("seq")
    head_devices = lax.axis_size("head")
    offsets = [2**s for s in range(block_lists.shape[1]) if 2**s < groups]
    count = len(offsets)
    reach = offsets[-1]
    hbm = pl.BlockSpec(memory_space=pl.ANY)
    vmem = pl.BlockSpec(memory_space=pltpu.VMEM)
    smem = pl.BlockSpec(memory_space=pltpu.SMEM)
    dma = pltpu.SemaphoreType.DMA
    return pl.pallas_call(
        functools.partial(kernel, groups, head_devices, offsets),
        out_shape=[jax.ShapeDtypeStruct((rows, feats), bf16)] * 5,
        in_specs=[hbm, hbm, hbm, vmem, vmem, vmem, smem, smem, vmem],
        out_specs=[vmem] * 5,
        scratch_shapes=[
            pltpu.VMEM((count + 1, rows, feats), bf16),
            pltpu.VMEM((count + 1, rows, feats), bf16),
            pltpu.VMEM((count + 1, rows, feats), bf16),
            pltpu.VMEM((count + 1, feats, rows), bf16),
            pltpu.VMEM((reach, 1, rows), jnp.int32),
            pltpu.VMEM((reach, 1, rows), jnp.int32),
            pltpu.VMEM((8, rows), f32),
            pltpu.VMEM((head_devices - 1, 8, rows), f32),
            pltpu.VMEM((count, rows, heads * rows), f32),
            pltpu.VMEM((count, rows, heads * rows), f32),
            pltpu.VMEM((count, rows, heads * rows), bf16),
            dma((3,)),
            dma((2, reach)),
            dma((2, reach)),
            dma((count,)),
            dma((count,)),
            dma((2, count)),
            dma((2, count)),
            dma((head_devices - 1,)),
            dma((head_devices - 1,)),
            dma((count,)),
            dma((count,)),
        ],
        compiler_params=pltpu.CompilerParams(
            collective_id=0, has_side_effects=True, vmem_limit_bytes=24 * 2**20
        ),
    )(
        query_rows,
        key_rows,
        value_rows,
        gate_rows,
        cotangent,
        event_gaps.reshape(1, rows),
        block_lists,
        bias_table,
        norm_gain.reshape(1, feats),
    )


def solution(mesh):
    placed = P("seq", "head")
    return jax.shard_map(
        per_device,
        mesh=mesh,
        in_specs=(
            placed,
            placed,
            placed,
            placed,
            placed,
            P("seq"),
            P(),
            P("head", None),
            P("head"),
        ),
        out_specs=(placed,) * 5,
        check_vma=False,
    )
```

```python
import functools

import jax
import jax.numpy as jnp
from jax import lax
from jax.experimental import pallas as pl
from jax.experimental.pallas import tpu as pltpu
from jax.sharding import PartitionSpec as P

norm_eps = 1e-05
f32 = jnp.float32
bf16 = jnp.bfloat16
MESH = pl.DeviceIdType.MESH


def mm(a, b):
    return lax.dot_general(a, b, (((1,), (0,)), ((), ())), preferred_element_type=f32)


def mm_nt(a, b):
    return lax.dot_general(a, b, (((1,), (1,)), ((), ())), preferred_element_type=f32)


def kernel(
    groups,
    head_devices,
    offsets,
    q_in,
    k_in,
    v_in,
    gate_in,
    cot_in,
    gaps_in,
    lists_in,
    table_in,
    gain_in,
    layer_ref,
    dq_ref,
    dk_ref,
    dv_ref,
    dgate_ref,
    gate_ref,
    cot_ref,
    gaps_ref,
    gain_ref,
    lists_ref,
    table_ref,
    qbuf,
    kbuf,
    vbuf,
    gabuf,
    gprev,
    glater,
    sums_out,
    sums_in,
    slope_q,
    slope_k,
    weight_k,
    att_acc,
    dq_acc,
    dk_acc,
    dv_acc,
    local_sem,
    gap_send,
    gap_recv,
    q_send,
    q_recv,
    kv_send,
    kv_recv,
    sum_send,
    sum_recv,
    ga_send,
    ga_recv,
):
    rows, feats = q_in.shape
    heads, buckets = table_in.shape
    head_dim = feats // heads
    scaling = head_dim**-0.5
    full_width = feats * head_devices
    reach = offsets[-1]
    count = len(offsets)
    me = lax.axis_index("seq")
    head = lax.axis_index("head")

    def to_later(d, body):
        pl.when(me + d < groups)(body)

    def to_earlier(d, body):
        pl.when(me >= d)(body)

    pairs = (
        (gaps_in, gaps_ref),
        (table_in, table_ref),
        (lists_in, lists_ref),
        (gain_in, gain_ref),
        (k_in, kbuf.at[0]),
        (q_in, qbuf.at[0]),
        (v_in, vbuf.at[0]),
        (gate_in, gate_ref),
        (cot_in, cot_ref),
    )
    own = [pltpu.make_async_copy(src, dst, local_sem.at[i]) for i, (src, dst) in enumerate(pairs)]
    for copy in own:
        copy.start()

    barrier = pltpu.get_barrier_semaphore()

    def greet(axis, where):
        pl.semaphore_signal(barrier, inc=1, device_id={axis: where}, device_id_type=MESH)

    for k in range(1, reach + 1):
        to_later(k, lambda k=k: greet("seq", me + k))
        to_earlier(k, lambda k=k: greet("seq", me - k))
    for r in range(1, head_devices):
        greet("head", lax.rem(head + r, head_devices))
    pl.semaphore_wait(
        barrier,
        jnp.minimum(me, reach) + jnp.minimum(groups - 1 - me, reach) + head_devices - 1,
    )

    def remote(src, dst, send, recv, axis, where):
        return pltpu.make_async_remote_copy(
            src_ref=src,
            dst_ref=dst,
            send_sem=send,
            recv_sem=recv,
            device_id={axis: where},
            device_id_type=MESH,
        )

    def gaps_up(k):
        return remote(
            gaps_in, gprev.at[k - 1], gap_send.at[0, k - 1], gap_recv.at[0, k - 1], "seq", me + k
        )

    def gaps_down(k):
        return remote(
            gaps_in, glater.at[k - 1], gap_send.at[1, k - 1], gap_recv.at[1, k - 1], "seq", me - k
        )

    def keys_up(s):
        return remote(
            k_in, kbuf.at[s + 1], kv_send.at[0, s], kv_recv.at[0, s], "seq", me + offsets[s]
        )

    def values_up(s):
        return remote(
            v_in, vbuf.at[s + 1], kv_send.at[1, s], kv_recv.at[1, s], "seq", me + offsets[s]
        )

    def queries_down(s):
        return remote(q_in, qbuf.at[s + 1], q_send.at[s], q_recv.at[s], "seq", me - offsets[s])

    def grads_down(s):
        return remote(
            gabuf.at[0], gabuf.at[s + 1], ga_send.at[s], ga_recv.at[s], "seq", me - offsets[s]
        )

    def sums_to(r):
        return remote(
            sums_out,
            sums_in.at[r - 1],
            sum_send.at[r - 1],
            sum_recv.at[r - 1],
            "head",
            lax.rem(head + r, head_devices),
        )

    for k in range(1, reach + 1):
        to_later(k, lambda k=k: gaps_up(k).start())
        to_earlier(k, lambda k=k: gaps_down(k).start())
    for s in range(count):
        to_later(offsets[s], lambda s=s: keys_up(s).start())
        to_later(offsets[s], lambda s=s: values_up(s).start())
        to_earlier(offsets[s], lambda s=s: queries_down(s).start())

    for k in range(1, reach + 1):

        def no_earlier(k=k):
            gprev[k - 1] = jnp.zeros_like(gprev[k - 1])

        def no_later(k=k):
            glater[k - 1] = jnp.zeros_like(glater[k - 1])

        pl.when(me < k)(no_earlier)
        pl.when(me + k >= groups)(no_later)

    row_ids = lax.broadcasted_iota(jnp.int32, (rows, rows), 0)
    col_ids = lax.broadcasted_iota(jnp.int32, (rows, rows), 1)
    upper = (row_ids <= col_ids).astype(f32)
    upper_bf = upper.astype(bf16)
    ones = jnp.ones((rows, rows), bf16)
    lane_head = lax.broadcasted_iota(jnp.int32, (rows, feats), 1) // head_dim
    sub_head = lax.broadcasted_iota(jnp.int32, (feats, rows), 0) // head_dim
    lane_masks = [(lane_head == h).astype(bf16) for h in range(heads)]
    sub_masks = [(sub_head == h).astype(bf16) for h in range(heads)]

    def prefix_row(gaps):
        wide = jnp.broadcast_to(gaps, (8, rows)).astype(bf16)
        return mm(wide, upper_bf)[0:1]

    def after_column(gaps):
        return mm(jnp.where(col_ids > row_ids, gaps, 0.0).astype(bf16), ones)

    def bias(delta):
        parts = [jnp.full(delta.shape, table_ref[h, 0], f32) for h in range(heads)]
        for b in range(1, buckets):
            reached = delta >= float(2 ** (b - 1))
            parts = [jnp.where(reached, table_ref[h, b], parts[h]) for h in range(heads)]
        return jnp.concatenate(parts, axis=1)

    def by_head_rows(q):
        return jnp.concatenate([q * mask for mask in lane_masks], axis=0)

    def by_head_lanes(g):
        return jnp.concatenate([g * mask for mask in sub_masks], axis=1)

    def own_heads(wide):
        return jnp.concatenate(
            [
                wide[h * head_dim : (h + 1) * head_dim, h * rows : (h + 1) * rows]
                for h in range(heads)
            ],
            axis=0,
        )

    def activate(keys, queries, biases, mask):
        scores = mm_nt(keys, queries) * scaling + biases
        sig = 0.5 * jnp.tanh(0.5 * scores) + 0.5
        weights = scores * sig
        slope = sig + weights * (1.0 - sig)
        return (weights * mask).astype(bf16), slope * mask

    for copy in own:
        copy.wait()
    own_gaps = gaps_ref[...].astype(f32)
    own_total = jnp.sum(own_gaps, axis=1, keepdims=True)
    own_row = prefix_row(own_gaps)
    own_after = after_column(own_gaps)
    diag_bias = bias(own_row + own_after - own_total)
    diag_mask = jnp.concatenate([upper] * heads, axis=1)
    gain = gain_ref[...]
    gates = gate_ref[...].astype(f32)
    upstream = cot_ref[...].astype(f32)
    scaled = (upstream * gates * gain).T

    keys = kbuf[0]
    values = vbuf[0]
    queries = by_head_rows(qbuf[0])
    diag_weights, diag_slope = activate(keys, queries, diag_bias, diag_mask)
    att_acc[...] = mm(values.T, diag_weights)

    for k in range(1, reach + 1):
        to_earlier(k, lambda k=k: gaps_up(k).wait_recv())
        to_later(k, lambda k=k: gaps_down(k).wait_recv())

    def between(buf, d):
        if d == 1:
            return jnp.zeros((1, 1), f32)
        return jnp.sum(
            jnp.sum(buf[0 : d - 1].astype(f32), axis=0), axis=1, keepdims=True
        )

    biases = []
    for s, d in enumerate(offsets):
        after = after_column(gprev[d - 1].astype(f32))
        biases.append(bias(own_row + after + between(gprev, d)))
    for s, d in enumerate(offsets):

        def attend(s=s):
            keys_up(s).wait_recv()
            listed = (lists_ref[me, s] >= 0).astype(f32)
            weights, slope = activate(kbuf[s + 1], queries, biases[s], listed)
            slope_q[s] = slope
            values_up(s).wait_recv()
            att_acc[...] += mm(vbuf[s + 1].T, weights)

        to_earlier(d, attend)

    flat = own_heads(att_acc[...])
    own_sums = [
        jnp.sum(x, axis=0, keepdims=True) for x in (flat, flat * flat, scaled, scaled * flat)
    ]
    sums_out[...] = jnp.concatenate(own_sums + [jnp.zeros((4, rows), f32)], axis=0)
    for r in range(1, head_devices):
        sums_to(r).start()

    for s, d in enumerate(offsets):

        def score_later(s=s, d=d):
            row = prefix_row(glater[d - 1].astype(f32))
            later_bias = bias(row + own_after + between(glater, d))
            listed = (lists_ref[me + d, s] >= 0).astype(f32)
            queries_down(s).wait_recv()
            weights, slope = activate(keys, by_head_rows(qbuf[s + 1]), later_bias, listed)
            weight_k[s] = weights
            slope_k[s] = slope

        to_later(d, score_later)

    for r in range(1, head_devices):
        sums_to(r).wait_recv()
    sums = sums_out[...]
    for r in range(1, head_devices):
        sums = sums + sums_in[r - 1]
    mean = sums[0:1] / full_width
    var = sums[1:2] / full_width - mean * mean
    inv_std = lax.rsqrt(var + norm_eps)
    centered = (flat - mean) * inv_std
    scaled_mean = sums[2:3] / full_width
    product_mean = inv_std * (sums[3:4] - mean * sums[2:3]) / full_width
    grad = (inv_std * (scaled - scaled_mean - centered * product_mean)).astype(bf16)
    gabuf[0] = grad
    for s in range(count):
        to_earlier(offsets[s], lambda s=s: grads_down(s).start())

    grads = by_head_lanes(grad)
    diag_grad = (mm(values, grads) * diag_slope).astype(bf16)
    dq_acc[...] = mm(keys.T, diag_grad)
    dk_acc[...] = mm(diag_grad, queries)
    dv_acc[...] = mm_nt(diag_weights, grads)
    for s, d in enumerate(offsets):

        def query_part(s=s):
            grad_scores = (mm(vbuf[s + 1], grads) * slope_q[s]).astype(bf16)
            dq_acc[...] += mm(kbuf[s + 1].T, grad_scores)

        to_earlier(d, query_part)
    dq_ref[...] = (own_heads(dq_acc[...]) * scaling).T.astype(bf16)
    normed = centered.T * gain
    layer_ref[...] = (normed * gates).astype(bf16)
    dgate_ref[...] = (upstream * normed).astype(bf16)

    for s, d in enumerate(offsets):

        def key_part(s=s):
            grads_down(s).wait_recv()
            grads = by_head_lanes(gabuf[s + 1])
            grad_scores = (mm(values, grads) * slope_k[s]).astype(bf16)
            dk_acc[...] += mm(grad_scores, by_head_rows(qbuf[s + 1]))
            dv_acc[...] += mm_nt(weight_k[s], grads)

        to_later(d, key_part)
    dk_ref[...] = (dk_acc[...] * scaling).astype(bf16)
    dv_ref[...] = dv_acc[...].astype(bf16)

    for k in range(1, reach + 1):
        to_later(k, lambda k=k: gaps_up(k).wait_send())
        to_earlier(k, lambda k=k: gaps_down(k).wait_send())
    for s, d in enumerate(offsets):
        to_later(d, lambda s=s: keys_up(s).wait_send())
        to_later(d, lambda s=s: values_up(s).wait_send())
        to_earlier(d, lambda s=s: queries_down(s).wait_send())
        to_earlier(d, lambda s=s: grads_down(s).wait_send())
    for r in range(1, head_devices):
        sums_to(r).wait_send()


def hand_out(*refs):
    sems = refs[-1]
    copies = [pltpu.make_async_copy(refs[i], refs[i + 5], sems.at[i]) for i in range(5)]
    for copy in copies:
        copy.start()
    for copy in copies:
        copy.wait()


def per_device(
    query_rows,
    key_rows,
    value_rows,
    gate_rows,
    cotangent,
    event_gaps,
    block_lists,
    bias_table,
    norm_gain,
):
    rows, feats = query_rows.shape
    heads = bias_table.shape[0]
    groups = lax.axis_size("seq")
    head_devices = lax.axis_size("head")
    offsets = [2**s for s in range(block_lists.shape[1]) if 2**s < groups]
    count = len(offsets)
    reach = offsets[-1]
    hbm = pl.BlockSpec(memory_space=pltpu.HBM)
    vmem = pl.BlockSpec(memory_space=pltpu.VMEM)
    dma = pltpu.SemaphoreType.DMA
    operands = (
        query_rows,
        key_rows,
        value_rows,
        gate_rows,
        cotangent,
        event_gaps.reshape(1, rows),
        block_lists,
        bias_table,
        norm_gain.reshape(1, feats),
    )
    results = pl.pallas_call(
        functools.partial(kernel, groups, head_devices, offsets),
        out_shape=[pltpu.VMEM((rows, feats), bf16)] * 5,
        in_specs=[hbm] * 9,
        out_specs=[vmem] * 5,
        scratch_shapes=[
            pltpu.VMEM((rows, feats), bf16),
            pltpu.VMEM((rows, feats), bf16),
            pltpu.VMEM((1, rows), jnp.int32),
            pltpu.VMEM((1, feats), f32),
            pltpu.SMEM(block_lists.shape, jnp.int32),
            pltpu.SMEM(bias_table.shape, f32),
            pltpu.VMEM((count + 1, rows, feats), bf16),
            pltpu.VMEM((count + 1, rows, feats), bf16),
            pltpu.VMEM((count + 1, rows, feats), bf16),
            pltpu.VMEM((count + 1, feats, rows), bf16),
            pltpu.VMEM((reach, 1, rows), jnp.int32),
            pltpu.VMEM((reach, 1, rows), jnp.int32),
            pltpu.VMEM((8, rows), f32),
            pltpu.VMEM((head_devices - 1, 8, rows), f32),
            pltpu.VMEM((count, rows, heads * rows), f32),
            pltpu.VMEM((count, rows, heads * rows), f32),
            pltpu.VMEM((count, rows, heads * rows), bf16),
            pltpu.VMEM((feats, heads * rows), f32),
            pltpu.VMEM((feats, heads * rows), f32),
            pltpu.VMEM((rows, feats), f32),
            pltpu.VMEM((rows, feats), f32),
            dma((9,)),
            dma((2, reach)),
            dma((2, reach)),
            dma((count,)),
            dma((count,)),
            dma((2, count)),
            dma((2, count)),
            dma((head_devices - 1,)),
            dma((head_devices - 1,)),
            dma((count,)),
            dma((count,)),
        ],
        compiler_params=pltpu.CompilerParams(
            collective_id=0, has_side_effects=True, vmem_limit_bytes=24 * 2**20
        ),
    )(*[pltpu.with_memory_space_constraint(x, pltpu.HBM) for x in operands])
    return pl.pallas_call(
        hand_out,
        out_shape=[jax.ShapeDtypeStruct((rows, feats), bf16)] * 5,
        in_specs=[vmem] * 5,
        out_specs=[hbm] * 5,
        scratch_shapes=[dma((5,))],
    )(*results)


def solution(mesh):
    placed = P("seq", "head")
    return jax.shard_map(
        per_device,
        mesh=mesh,
        in_specs=(
            placed,
            placed,
            placed,
            placed,
            placed,
            P("seq"),
            P(),
            P("head", None),
            P("head"),
        ),
        out_specs=(placed,) * 5,
        check_vma=False,
    )
```

```python
import functools

import jax
import jax.numpy as jnp
from jax import lax
from jax.experimental import pallas as pl
from jax.experimental.pallas import tpu as pltpu
from jax.sharding import PartitionSpec as P

norm_eps = 1e-05
f32 = jnp.float32
bf16 = jnp.bfloat16
MESH = pl.DeviceIdType.MESH


def mm(a, b):
    return lax.dot_general(a, b, (((1,), (0,)), ((), ())), preferred_element_type=f32)


def mm_nt(a, b):
    return lax.dot_general(a, b, (((1,), (1,)), ((), ())), preferred_element_type=f32)


def kernel(
    groups,
    head_devices,
    offsets,
    q_in,
    k_in,
    v_in,
    gate_in,
    cot_in,
    gaps_in,
    lists_in,
    table_in,
    gain_in,
    layer_ref,
    dq_ref,
    dk_ref,
    dv_ref,
    dgate_ref,
    gate_ref,
    cot_ref,
    gaps_ref,
    gain_ref,
    lists_ref,
    table_ref,
    qbuf,
    kbuf,
    vbuf,
    gabuf,
    gprev,
    glater,
    sums_out,
    sums_in,
    slope_q,
    slope_k,
    weight_k,
    att_acc,
    dq_acc,
    dk_acc,
    dv_acc,
    local_sem,
    gap_send,
    gap_recv,
    q_send,
    q_recv,
    kv_send,
    kv_recv,
    sum_send,
    sum_recv,
    ga_send,
    ga_recv,
):
    rows, feats = q_in.shape
    heads, buckets = table_in.shape
    head_dim = feats // heads
    scaling = head_dim**-0.5
    full_width = feats * head_devices
    reach = offsets[-1]
    count = len(offsets)
    me = lax.axis_index("seq")
    head = lax.axis_index("head")

    def to_later(d, body):
        pl.when(me + d < groups)(body)

    def to_earlier(d, body):
        pl.when(me >= d)(body)

    pairs = (
        (gaps_in, gaps_ref),
        (table_in, table_ref),
        (lists_in, lists_ref),
        (gain_in, gain_ref),
        (k_in, kbuf.at[0]),
        (q_in, qbuf.at[0]),
        (v_in, vbuf.at[0]),
        (gate_in, gate_ref),
        (cot_in, cot_ref),
    )
    own = [pltpu.make_async_copy(src, dst, local_sem.at[i]) for i, (src, dst) in enumerate(pairs)]
    for copy in own:
        copy.start()

    barrier = pltpu.get_barrier_semaphore()

    def greet(axis, where):
        pl.semaphore_signal(barrier, inc=1, device_id={axis: where}, device_id_type=MESH)

    for k in range(1, reach + 1):
        to_later(k, lambda k=k: greet("seq", me + k))
        to_earlier(k, lambda k=k: greet("seq", me - k))
    for r in range(1, head_devices):
        greet("head", lax.rem(head + r, head_devices))
    pl.semaphore_wait(
        barrier,
        jnp.minimum(me, reach) + jnp.minimum(groups - 1 - me, reach) + head_devices - 1,
    )

    def remote(src, dst, send, recv, axis, where):
        return pltpu.make_async_remote_copy(
            src_ref=src,
            dst_ref=dst,
            send_sem=send,
            recv_sem=recv,
            device_id={axis: where},
            device_id_type=MESH,
        )

    def gaps_up(k):
        return remote(
            gaps_in, gprev.at[k - 1], gap_send.at[0, k - 1], gap_recv.at[0, k - 1], "seq", me + k
        )

    def gaps_down(k):
        return remote(
            gaps_in, glater.at[k - 1], gap_send.at[1, k - 1], gap_recv.at[1, k - 1], "seq", me - k
        )

    def keys_up(s):
        return remote(
            k_in, kbuf.at[s + 1], kv_send.at[0, s], kv_recv.at[0, s], "seq", me + offsets[s]
        )

    def values_up(s):
        return remote(
            v_in, vbuf.at[s + 1], kv_send.at[1, s], kv_recv.at[1, s], "seq", me + offsets[s]
        )

    def queries_down(s):
        return remote(q_in, qbuf.at[s + 1], q_send.at[s], q_recv.at[s], "seq", me - offsets[s])

    def grads_down(s):
        return remote(
            gabuf.at[0], gabuf.at[s + 1], ga_send.at[s], ga_recv.at[s], "seq", me - offsets[s]
        )

    def sums_to(r):
        return remote(
            sums_out,
            sums_in.at[r - 1],
            sum_send.at[r - 1],
            sum_recv.at[r - 1],
            "head",
            lax.rem(head + r, head_devices),
        )

    for k in range(1, reach + 1):
        to_later(k, lambda k=k: gaps_up(k).start())
        to_earlier(k, lambda k=k: gaps_down(k).start())
    for s in range(count):
        to_later(offsets[s], lambda s=s: keys_up(s).start())
        to_later(offsets[s], lambda s=s: values_up(s).start())
        to_earlier(offsets[s], lambda s=s: queries_down(s).start())

    for k in range(1, reach + 1):

        def no_earlier(k=k):
            gprev[k - 1] = jnp.zeros_like(gprev[k - 1])

        def no_later(k=k):
            glater[k - 1] = jnp.zeros_like(glater[k - 1])

        pl.when(me < k)(no_earlier)
        pl.when(me + k >= groups)(no_later)

    row_ids = lax.broadcasted_iota(jnp.int32, (rows, rows), 0)
    col_ids = lax.broadcasted_iota(jnp.int32, (rows, rows), 1)
    upper = (row_ids <= col_ids).astype(f32)
    upper_bf = upper.astype(bf16)
    ones = jnp.ones((rows, rows), bf16)
    lane_head = lax.broadcasted_iota(jnp.int32, (rows, feats), 1) // head_dim
    sub_head = lax.broadcasted_iota(jnp.int32, (feats, rows), 0) // head_dim
    lane_masks = [(lane_head == h).astype(bf16) for h in range(heads)]
    sub_masks = [(sub_head == h).astype(bf16) for h in range(heads)]

    def prefix_row(gaps):
        wide = jnp.broadcast_to(gaps, (8, rows)).astype(bf16)
        return mm(wide, upper_bf)[0:1]

    def after_column(gaps):
        return mm(jnp.where(col_ids > row_ids, gaps, 0.0).astype(bf16), ones)

    def bias(delta):
        parts = [jnp.full(delta.shape, table_ref[h, 0], f32) for h in range(heads)]
        for b in range(1, buckets):
            reached = delta >= float(2 ** (b - 1))
            parts = [jnp.where(reached, table_ref[h, b], parts[h]) for h in range(heads)]
        return jnp.concatenate(parts, axis=1)

    def by_head_rows(q):
        return jnp.concatenate([q * mask for mask in lane_masks], axis=0)

    def by_head_lanes(g):
        return jnp.concatenate([g * mask for mask in sub_masks], axis=1)

    def own_heads(wide):
        return jnp.concatenate(
            [
                wide[h * head_dim : (h + 1) * head_dim, h * rows : (h + 1) * rows]
                for h in range(heads)
            ],
            axis=0,
        )

    def activate(keys, queries, biases, mask):
        scores = mm_nt(keys, queries) * scaling + biases
        sig = 0.5 * jnp.tanh(0.5 * scores) + 0.5
        weights = scores * sig
        slope = sig + weights * (1.0 - sig)
        return (weights * mask).astype(bf16), slope * mask

    for copy in own:
        copy.wait()
    own_gaps = gaps_ref[...].astype(f32)
    own_total = jnp.sum(own_gaps, axis=1, keepdims=True)
    own_row = prefix_row(own_gaps)
    own_after = after_column(own_gaps)
    diag_bias = bias(own_row + own_after - own_total)
    diag_mask = jnp.concatenate([upper] * heads, axis=1)
    gain = gain_ref[...]
    gates = gate_ref[...].astype(f32)
    upstream = cot_ref[...].astype(f32)
    scaled = (upstream * gates * gain).T

    keys = kbuf[0]
    values = vbuf[0]
    queries = by_head_rows(qbuf[0])
    diag_weights, diag_slope = activate(keys, queries, diag_bias, diag_mask)
    att_acc[...] = mm(values.T, diag_weights)

    for k in range(1, reach + 1):
        to_earlier(k, lambda k=k: gaps_up(k).wait_recv())
        to_later(k, lambda k=k: gaps_down(k).wait_recv())

    def between(buf, d):
        if d == 1:
            return jnp.zeros((1, 1), f32)
        return jnp.sum(
            jnp.sum(buf[0 : d - 1].astype(f32), axis=0), axis=1, keepdims=True
        )

    biases = []
    for s, d in enumerate(offsets):
        after = after_column(gprev[d - 1].astype(f32))
        biases.append(bias(own_row + after + between(gprev, d)))
    for s, d in enumerate(offsets):

        def score_later(s=s, d=d):
            row = prefix_row(glater[d - 1].astype(f32))
            later_bias = bias(row + own_after + between(glater, d))
            listed = (lists_ref[me + d, s] >= 0).astype(f32)
            queries_down(s).wait_recv()
            weights, slope = activate(keys, by_head_rows(qbuf[s + 1]), later_bias, listed)
            weight_k[s] = weights
            slope_k[s] = slope

        to_later(d, score_later)

    for s, d in enumerate(offsets):

        def attend(s=s):
            keys_up(s).wait_recv()
            listed = (lists_ref[me, s] >= 0).astype(f32)
            weights, slope = activate(kbuf[s + 1], queries, biases[s], listed)
            slope_q[s] = slope
            values_up(s).wait_recv()
            att_acc[...] += mm(vbuf[s + 1].T, weights)

        to_earlier(d, attend)

    flat = own_heads(att_acc[...])
    own_sums = [
        jnp.sum(x, axis=0, keepdims=True) for x in (flat, flat * flat, scaled, scaled * flat)
    ]
    sums_out[...] = jnp.concatenate(own_sums + [jnp.zeros((4, rows), f32)], axis=0)
    for r in range(1, head_devices):
        sums_to(r).start()

    for r in range(1, head_devices):
        sums_to(r).wait_recv()
    sums = sums_out[...]
    for r in range(1, head_devices):
        sums = sums + sums_in[r - 1]
    mean = sums[0:1] / full_width
    var = sums[1:2] / full_width - mean * mean
    inv_std = lax.rsqrt(var + norm_eps)
    centered = (flat - mean) * inv_std
    scaled_mean = sums[2:3] / full_width
    product_mean = inv_std * (sums[3:4] - mean * sums[2:3]) / full_width
    grad = (inv_std * (scaled - scaled_mean - centered * product_mean)).astype(bf16)
    gabuf[0] = grad
    for s in range(count):
        to_earlier(offsets[s], lambda s=s: grads_down(s).start())

    grads = by_head_lanes(grad)
    diag_grad = (mm(values, grads) * diag_slope).astype(bf16)
    dq_acc[...] = mm(keys.T, diag_grad)
    dk_acc[...] = mm(diag_grad, queries)
    dv_acc[...] = mm_nt(diag_weights, grads)
    for s, d in enumerate(offsets):

        def query_part(s=s):
            grad_scores = (mm(vbuf[s + 1], grads) * slope_q[s]).astype(bf16)
            dq_acc[...] += mm(kbuf[s + 1].T, grad_scores)

        to_earlier(d, query_part)
    dq_ref[...] = (own_heads(dq_acc[...]) * scaling).T.astype(bf16)
    normed = centered.T * gain
    layer_ref[...] = (normed * gates).astype(bf16)
    dgate_ref[...] = (upstream * normed).astype(bf16)

    for s, d in enumerate(offsets):

        def key_part(s=s):
            grads_down(s).wait_recv()
            grads = by_head_lanes(gabuf[s + 1])
            grad_scores = (mm(values, grads) * slope_k[s]).astype(bf16)
            dk_acc[...] += mm(grad_scores, by_head_rows(qbuf[s + 1]))
            dv_acc[...] += mm_nt(weight_k[s], grads)

        to_later(d, key_part)
    dk_ref[...] = (dk_acc[...] * scaling).astype(bf16)
    dv_ref[...] = dv_acc[...].astype(bf16)

    for k in range(1, reach + 1):
        to_later(k, lambda k=k: gaps_up(k).wait_send())
        to_earlier(k, lambda k=k: gaps_down(k).wait_send())
    for s, d in enumerate(offsets):
        to_later(d, lambda s=s: keys_up(s).wait_send())
        to_later(d, lambda s=s: values_up(s).wait_send())
        to_earlier(d, lambda s=s: queries_down(s).wait_send())
        to_earlier(d, lambda s=s: grads_down(s).wait_send())
    for r in range(1, head_devices):
        sums_to(r).wait_send()


def hand_out(*refs):
    sems = refs[-1]
    copies = [pltpu.make_async_copy(refs[i], refs[i + 5], sems.at[i]) for i in range(5)]
    for copy in copies:
        copy.start()
    for copy in copies:
        copy.wait()


def per_device(
    query_rows,
    key_rows,
    value_rows,
    gate_rows,
    cotangent,
    event_gaps,
    block_lists,
    bias_table,
    norm_gain,
):
    rows, feats = query_rows.shape
    heads = bias_table.shape[0]
    groups = lax.axis_size("seq")
    head_devices = lax.axis_size("head")
    offsets = [2**s for s in range(block_lists.shape[1]) if 2**s < groups]
    count = len(offsets)
    reach = offsets[-1]
    hbm = pl.BlockSpec(memory_space=pltpu.HBM)
    vmem = pl.BlockSpec(memory_space=pltpu.VMEM)
    dma = pltpu.SemaphoreType.DMA
    operands = (
        query_rows,
        key_rows,
        value_rows,
        gate_rows,
        cotangent,
        event_gaps.reshape(1, rows),
        block_lists,
        bias_table,
        norm_gain.reshape(1, feats),
    )
    results = pl.pallas_call(
        functools.partial(kernel, groups, head_devices, offsets),
        out_shape=[pltpu.VMEM((rows, feats), bf16)] * 5,
        in_specs=[hbm] * 9,
        out_specs=[vmem] * 5,
        scratch_shapes=[
            pltpu.VMEM((rows, feats), bf16),
            pltpu.VMEM((rows, feats), bf16),
            pltpu.VMEM((1, rows), jnp.int32),
            pltpu.VMEM((1, feats), f32),
            pltpu.SMEM(block_lists.shape, jnp.int32),
            pltpu.SMEM(bias_table.shape, f32),
            pltpu.VMEM((count + 1, rows, feats), bf16),
            pltpu.VMEM((count + 1, rows, feats), bf16),
            pltpu.VMEM((count + 1, rows, feats), bf16),
            pltpu.VMEM((count + 1, feats, rows), bf16),
            pltpu.VMEM((reach, 1, rows), jnp.int32),
            pltpu.VMEM((reach, 1, rows), jnp.int32),
            pltpu.VMEM((8, rows), f32),
            pltpu.VMEM((head_devices - 1, 8, rows), f32),
            pltpu.VMEM((count, rows, heads * rows), f32),
            pltpu.VMEM((count, rows, heads * rows), f32),
            pltpu.VMEM((count, rows, heads * rows), bf16),
            pltpu.VMEM((feats, heads * rows), f32),
            pltpu.VMEM((feats, heads * rows), f32),
            pltpu.VMEM((rows, feats), f32),
            pltpu.VMEM((rows, feats), f32),
            dma((9,)),
            dma((2, reach)),
            dma((2, reach)),
            dma((count,)),
            dma((count,)),
            dma((2, count)),
            dma((2, count)),
            dma((head_devices - 1,)),
            dma((head_devices - 1,)),
            dma((count,)),
            dma((count,)),
        ],
        compiler_params=pltpu.CompilerParams(
            collective_id=0, has_side_effects=True, vmem_limit_bytes=24 * 2**20
        ),
    )(*[pltpu.with_memory_space_constraint(x, pltpu.HBM) for x in operands])
    return pl.pallas_call(
        hand_out,
        out_shape=[jax.ShapeDtypeStruct((rows, feats), bf16)] * 5,
        in_specs=[vmem] * 5,
        out_specs=[hbm] * 5,
        scratch_shapes=[dma((5,))],
        compiler_params=pltpu.CompilerParams(vmem_limit_bytes=2**20),
    )(*[pltpu.with_memory_space_constraint(x, pltpu.VMEM) for x in results])


def solution(mesh):
    placed = P("seq", "head")
    return jax.shard_map(
        per_device,
        mesh=mesh,
        in_specs=(
            placed,
            placed,
            placed,
            placed,
            placed,
            P("seq"),
            P(),
            P("head", None),
            P("head"),
        ),
        out_specs=(placed,) * 5,
        check_vma=False,
    )
```

```python
import functools

import jax
import jax.numpy as jnp
from jax import lax
from jax.experimental import pallas as pl
from jax.experimental.pallas import tpu as pltpu
from jax.sharding import PartitionSpec as P

norm_eps = 1e-05
f32 = jnp.float32
bf16 = jnp.bfloat16
MESH = pl.DeviceIdType.MESH


def mm(a, b):
    return lax.dot_general(a, b, (((1,), (0,)), ((), ())), preferred_element_type=f32)


def mm_nt(a, b):
    return lax.dot_general(a, b, (((1,), (1,)), ((), ())), preferred_element_type=f32)


def kernel(
    groups,
    head_devices,
    offsets,
    q_in,
    k_in,
    v_in,
    gate_in,
    cot_in,
    gaps_in,
    lists_in,
    table_in,
    gain_in,
    layer_ref,
    dq_ref,
    dk_ref,
    dv_ref,
    dgate_ref,
    gate_ref,
    cot_ref,
    gaps_ref,
    gain_ref,
    lists_ref,
    table_ref,
    qbuf,
    kbuf,
    vbuf,
    gabuf,
    gprev,
    glater,
    sums_out,
    sums_in,
    slope_q,
    slope_k,
    weight_k,
    att_acc,
    dq_acc,
    dk_acc,
    dv_acc,
    local_sem,
    gap_send,
    gap_recv,
    q_send,
    q_recv,
    kv_send,
    kv_recv,
    sum_send,
    sum_recv,
    ga_send,
    ga_recv,
):
    rows, feats = q_in.shape
    heads, buckets = table_in.shape
    head_dim = feats // heads
    scaling = head_dim**-0.5
    full_width = feats * head_devices
    reach = offsets[-1]
    count = len(offsets)
    me = lax.axis_index("seq")
    head = lax.axis_index("head")

    def to_later(d, body):
        pl.when(me + d < groups)(body)

    def to_earlier(d, body):
        pl.when(me >= d)(body)

    pairs = (
        (k_in, kbuf.at[0]),
        (v_in, vbuf.at[0]),
        (gaps_in, gaps_ref),
        (table_in, table_ref),
        (lists_in, lists_ref),
        (gain_in, gain_ref),
        (q_in, qbuf.at[0]),
        (gate_in, gate_ref),
        (cot_in, cot_ref),
    )
    own = [pltpu.make_async_copy(src, dst, local_sem.at[i]) for i, (src, dst) in enumerate(pairs)]
    for copy in own:
        copy.start()

    barrier = pltpu.get_barrier_semaphore()

    def greet(axis, where):
        pl.semaphore_signal(barrier, inc=1, device_id={axis: where}, device_id_type=MESH)

    for k in range(1, reach + 1):
        to_later(k, lambda k=k: greet("seq", me + k))
        to_earlier(k, lambda k=k: greet("seq", me - k))
    for r in range(1, head_devices):
        greet("head", lax.rem(head + r, head_devices))
    pl.semaphore_wait(
        barrier,
        jnp.minimum(me, reach) + jnp.minimum(groups - 1 - me, reach) + head_devices - 1,
    )

    other_group = lax.rem(me + 1, groups)

    def remote(src, dst, send, recv, axis, where):
        return pltpu.make_async_remote_copy(
            src_ref=src,
            dst_ref=dst,
            send_sem=send,
            recv_sem=recv,
            device_id={axis: where},
            device_id_type=MESH,
        )

    def gaps_up(k):
        return remote(
            gaps_in, gprev.at[k - 1], gap_send.at[0, k - 1], gap_recv.at[0, k - 1], "seq", me + k
        )

    def gaps_down(k):
        return remote(
            gaps_in, glater.at[k - 1], gap_send.at[1, k - 1], gap_recv.at[1, k - 1], "seq", me - k
        )

    def block_copy(buf, which, source, s, where):
        return remote(
            buf.at[source],
            buf.at[s + 1],
            kv_send.at[which, s],
            kv_recv.at[which, s],
            "seq",
            where,
        )

    def pass_up(which, source, s, where):
        block_copy((kbuf, vbuf)[which], which, source, s, where).start()

    def first_up(which):
        near = (me % 2 == 0) & (me + 1 < groups)
        if count > 1:
            pl.when(me + 2 < groups)(lambda: pass_up(which, 0, 1, me + 2))
        pl.when(near)(lambda: pass_up(which, 0, 0, me + 1))

    def relay_up(which, s):
        if s == 1:
            pl.when((me % 2 == 1) & (me >= 2))(lambda: pass_up(which, 2, 0, me - 1))
        if 1 <= s < count - 1:
            step = offsets[s]
            pl.when((me >= step) & (me + step < groups))(
                lambda: pass_up(which, s + 1, s + 1, me + step)
            )

    def wait_block(which, s):
        block_copy((kbuf, vbuf)[which], which, 0, s, other_group).wait_recv()

    def wait_block_sent(which, s):
        block_copy((kbuf, vbuf)[which], which, 0, s, other_group).wait_send()

    def queries_down(s):
        return remote(q_in, qbuf.at[s + 1], q_send.at[s], q_recv.at[s], "seq", me - offsets[s])

    def grads_copy(source, s, where):
        return remote(
            gabuf.at[source], gabuf.at[s + 1], ga_send.at[s], ga_recv.at[s], "seq", where
        )

    def first_down():
        if count > 1:
            pl.when(me >= 2)(lambda: grads_copy(0, 1, me - 2).start())
        pl.when(me % 2 == 1)(lambda: grads_copy(0, 0, me - 1).start())

    def relay_down(s):
        if s == 1:
            pl.when((me % 2 == 0) & (me + 2 < groups))(
                lambda: grads_copy(2, 0, me + 1).start()
            )
        if 1 <= s < count - 1:
            step = offsets[s]
            pl.when((me >= step) & (me + step < groups))(
                lambda: grads_copy(s + 1, s + 1, me - step).start()
            )

    def sums_to(r):
        return remote(
            sums_out,
            sums_in.at[r - 1],
            sum_send.at[r - 1],
            sum_recv.at[r - 1],
            "head",
            lax.rem(head + r, head_devices),
        )

    for k in range(1, reach + 1):
        to_later(k, lambda k=k: gaps_up(k).start())
        to_earlier(k, lambda k=k: gaps_down(k).start())
    own[0].wait()
    own[1].wait()
    first_up(0)
    first_up(1)
    for s in range(count):
        to_earlier(offsets[s], lambda s=s: queries_down(s).start())

    for k in range(1, reach + 1):

        def no_earlier(k=k):
            gprev[k - 1] = jnp.zeros_like(gprev[k - 1])

        def no_later(k=k):
            glater[k - 1] = jnp.zeros_like(glater[k - 1])

        pl.when(me < k)(no_earlier)
        pl.when(me + k >= groups)(no_later)

    row_ids = lax.broadcasted_iota(jnp.int32, (rows, rows), 0)
    col_ids = lax.broadcasted_iota(jnp.int32, (rows, rows), 1)
    upper = (row_ids <= col_ids).astype(f32)
    upper_bf = upper.astype(bf16)
    ones = jnp.ones((rows, rows), bf16)
    lane_head = lax.broadcasted_iota(jnp.int32, (rows, feats), 1) // head_dim
    sub_head = lax.broadcasted_iota(jnp.int32, (feats, rows), 0) // head_dim
    lane_masks = [(lane_head == h).astype(bf16) for h in range(heads)]
    sub_masks = [(sub_head == h).astype(bf16) for h in range(heads)]

    def prefix_row(gaps):
        wide = jnp.broadcast_to(gaps, (8, rows)).astype(bf16)
        return mm(wide, upper_bf)[0:1]

    def after_column(gaps):
        return mm(jnp.where(col_ids > row_ids, gaps, 0.0).astype(bf16), ones)

    def bias(delta):
        parts = [jnp.full(delta.shape, table_ref[h, 0], f32) for h in range(heads)]
        for b in range(1, buckets):
            reached = delta >= float(2 ** (b - 1))
            parts = [jnp.where(reached, table_ref[h, b], parts[h]) for h in range(heads)]
        return jnp.concatenate(parts, axis=1)

    def by_head_rows(q):
        return jnp.concatenate([q * mask for mask in lane_masks], axis=0)

    def by_head_lanes(g):
        return jnp.concatenate([g * mask for mask in sub_masks], axis=1)

    def own_heads(wide):
        return jnp.concatenate(
            [
                wide[h * head_dim : (h + 1) * head_dim, h * rows : (h + 1) * rows]
                for h in range(heads)
            ],
            axis=0,
        )

    def activate(keys, queries, biases, mask):
        scores = mm_nt(keys, queries) * scaling + biases
        sig = 0.5 * jnp.tanh(0.5 * scores) + 0.5
        weights = scores * sig
        slope = sig + weights * (1.0 - sig)
        return (weights * mask).astype(bf16), slope * mask

    for copy in own[2:]:
        copy.wait()
    own_gaps = gaps_ref[...].astype(f32)
    own_total = jnp.sum(own_gaps, axis=1, keepdims=True)
    own_row = prefix_row(own_gaps)
    own_after = after_column(own_gaps)
    diag_bias = bias(own_row + own_after - own_total)
    diag_mask = jnp.concatenate([upper] * heads, axis=1)
    gain = gain_ref[...]
    gates = gate_ref[...].astype(f32)
    upstream = cot_ref[...].astype(f32)
    scaled = (upstream * gates * gain).T

    keys = kbuf[0]
    values = vbuf[0]
    queries = by_head_rows(qbuf[0])
    diag_weights, diag_slope = activate(keys, queries, diag_bias, diag_mask)
    att_acc[...] = mm(values.T, diag_weights)

    def receive(s):
        for which in range(2):

            def arrived(which=which):
                wait_block(which, s)
                relay_up(which, s)

            to_earlier(offsets[s], arrived)

    for k in range(1, reach + 1):
        to_earlier(k, lambda k=k: gaps_up(k).wait_recv())
        to_later(k, lambda k=k: gaps_down(k).wait_recv())

    def between(buf, d):
        if d == 1:
            return jnp.zeros((1, 1), f32)
        return jnp.sum(
            jnp.sum(buf[0 : d - 1].astype(f32), axis=0), axis=1, keepdims=True
        )

    biases = []
    for s, d in enumerate(offsets):
        after = after_column(gprev[d - 1].astype(f32))
        biases.append(bias(own_row + after + between(gprev, d)))
    if count > 1:
        receive(1)

    for s, d in enumerate(offsets):

        def score_later(s=s, d=d):
            row = prefix_row(glater[d - 1].astype(f32))
            later_bias = bias(row + own_after + between(glater, d))
            listed = (lists_ref[me + d, s] >= 0).astype(f32)
            queries_down(s).wait_recv()
            weights, slope = activate(keys, by_head_rows(qbuf[s + 1]), later_bias, listed)
            weight_k[s] = weights
            slope_k[s] = slope

        to_later(d, score_later)

    order = [s for s in (1, 0) if s < count] + list(range(2, count))
    for s in order:
        d = offsets[s]
        if s != 1:
            receive(s)

        def attend(s=s):
            listed = (lists_ref[me, s] >= 0).astype(f32)
            weights, slope = activate(kbuf[s + 1], queries, biases[s], listed)
            slope_q[s] = slope
            att_acc[...] += mm(vbuf[s + 1].T, weights)

        to_earlier(d, attend)

    flat = own_heads(att_acc[...])
    own_sums = [
        jnp.sum(x, axis=0, keepdims=True) for x in (flat, flat * flat, scaled, scaled * flat)
    ]
    sums_out[...] = jnp.concatenate(own_sums + [jnp.zeros((4, rows), f32)], axis=0)
    for r in range(1, head_devices):
        sums_to(r).start()

    for r in range(1, head_devices):
        sums_to(r).wait_recv()
    sums = sums_out[...]
    for r in range(1, head_devices):
        sums = sums + sums_in[r - 1]
    mean = sums[0:1] / full_width
    var = sums[1:2] / full_width - mean * mean
    inv_std = lax.rsqrt(var + norm_eps)
    centered = (flat - mean) * inv_std
    scaled_mean = sums[2:3] / full_width
    product_mean = inv_std * (sums[3:4] - mean * sums[2:3]) / full_width
    grad = (inv_std * (scaled - scaled_mean - centered * product_mean)).astype(bf16)
    gabuf[0] = grad
    first_down()

    grads = by_head_lanes(grad)
    diag_grad = (mm(values, grads) * diag_slope).astype(bf16)
    dq_acc[...] = mm(keys.T, diag_grad)
    dk_acc[...] = mm(diag_grad, queries)
    dv_acc[...] = mm_nt(diag_weights, grads)
    for s, d in enumerate(offsets):

        def query_part(s=s):
            grad_scores = (mm(vbuf[s + 1], grads) * slope_q[s]).astype(bf16)
            dq_acc[...] += mm(kbuf[s + 1].T, grad_scores)

        to_earlier(d, query_part)
    def receive_grads(s):
        def arrived():
            grads_copy(0, s, other_group).wait_recv()
            relay_down(s)

        to_later(offsets[s], arrived)

    if count > 1:
        receive_grads(1)
    dq_ref[...] = (own_heads(dq_acc[...]) * scaling).T.astype(bf16)
    normed = centered.T * gain
    layer_ref[...] = (normed * gates).astype(bf16)
    dgate_ref[...] = (upstream * normed).astype(bf16)

    for s in order:
        d = offsets[s]
        if s != 1:
            receive_grads(s)

        def key_part(s=s):
            grads = by_head_lanes(gabuf[s + 1])
            grad_scores = (mm(values, grads) * slope_k[s]).astype(bf16)
            dk_acc[...] += mm(grad_scores, by_head_rows(qbuf[s + 1]))
            dv_acc[...] += mm_nt(weight_k[s], grads)

        to_later(d, key_part)
    dk_ref[...] = (dk_acc[...] * scaling).astype(bf16)
    dv_ref[...] = dv_acc[...].astype(bf16)

    for k in range(1, reach + 1):
        to_later(k, lambda k=k: gaps_up(k).wait_send())
        to_earlier(k, lambda k=k: gaps_down(k).wait_send())
    for s, d in enumerate(offsets):
        if s == 0:
            sent_up = ((me % 2 == 0) & (me + 1 < groups)) | ((me % 2 == 1) & (me >= 2))
            sent_down = (me % 2 == 1) | ((me % 2 == 0) & (me + 2 < groups))
        elif s == 1:
            sent_up = me + 2 < groups
            sent_down = me >= 2
        else:
            sent_up = (me >= d // 2) & (me + d // 2 < groups)
            sent_down = sent_up
        for which in range(2):
            pl.when(sent_up)(lambda which=which, s=s: wait_block_sent(which, s))
        to_earlier(d, lambda s=s: queries_down(s).wait_send())
        pl.when(sent_down)(lambda s=s: grads_copy(0, s, other_group).wait_send())
    for r in range(1, head_devices):
        sums_to(r).wait_send()


def hand_out(*refs):
    sems = refs[-1]
    copies = [pltpu.make_async_copy(refs[i], refs[i + 5], sems.at[i]) for i in range(5)]
    for copy in copies:
        copy.start()
    for copy in copies:
        copy.wait()


def per_device(
    query_rows,
    key_rows,
    value_rows,
    gate_rows,
    cotangent,
    event_gaps,
    block_lists,
    bias_table,
    norm_gain,
):
    rows, feats = query_rows.shape
    heads = bias_table.shape[0]
    groups = lax.axis_size("seq")
    head_devices = lax.axis_size("head")
    offsets = [2**s for s in range(block_lists.shape[1]) if 2**s < groups]
    count = len(offsets)
    reach = offsets[-1]
    hbm = pl.BlockSpec(memory_space=pltpu.HBM)
    vmem = pl.BlockSpec(memory_space=pltpu.VMEM)
    dma = pltpu.SemaphoreType.DMA
    operands = (
        query_rows,
        key_rows,
        value_rows,
        gate_rows,
        cotangent,
        event_gaps.reshape(1, rows),
        block_lists,
        bias_table,
        norm_gain.reshape(1, feats),
    )
    results = pl.pallas_call(
        functools.partial(kernel, groups, head_devices, offsets),
        out_shape=[pltpu.VMEM((rows, feats), bf16)] * 5,
        in_specs=[hbm] * 9,
        out_specs=[vmem] * 5,
        scratch_shapes=[
            pltpu.VMEM((rows, feats), bf16),
            pltpu.VMEM((rows, feats), bf16),
            pltpu.VMEM((1, rows), jnp.int32),
            pltpu.VMEM((1, feats), f32),
            pltpu.SMEM(block_lists.shape, jnp.int32),
            pltpu.SMEM(bias_table.shape, f32),
            pltpu.VMEM((count + 1, rows, feats), bf16),
            pltpu.VMEM((count + 1, rows, feats), bf16),
            pltpu.VMEM((count + 1, rows, feats), bf16),
            pltpu.VMEM((count + 1, feats, rows), bf16),
            pltpu.VMEM((reach, 1, rows), jnp.int32),
            pltpu.VMEM((reach, 1, rows), jnp.int32),
            pltpu.VMEM((8, rows), f32),
            pltpu.VMEM((head_devices - 1, 8, rows), f32),
            pltpu.VMEM((count, rows, heads * rows), f32),
            pltpu.VMEM((count, rows, heads * rows), f32),
            pltpu.VMEM((count, rows, heads * rows), bf16),
            pltpu.VMEM((feats, heads * rows), f32),
            pltpu.VMEM((feats, heads * rows), f32),
            pltpu.VMEM((rows, feats), f32),
            pltpu.VMEM((rows, feats), f32),
            dma((9,)),
            dma((2, reach)),
            dma((2, reach)),
            dma((count,)),
            dma((count,)),
            dma((2, count)),
            dma((2, count)),
            dma((head_devices - 1,)),
            dma((head_devices - 1,)),
            dma((count,)),
            dma((count,)),
        ],
        compiler_params=pltpu.CompilerParams(
            collective_id=0, has_side_effects=True, vmem_limit_bytes=24 * 2**20
        ),
    )(*[pltpu.with_memory_space_constraint(x, pltpu.HBM) for x in operands])
    return pl.pallas_call(
        hand_out,
        out_shape=[jax.ShapeDtypeStruct((rows, feats), bf16)] * 5,
        in_specs=[vmem] * 5,
        out_specs=[hbm] * 5,
        scratch_shapes=[dma((5,))],
        compiler_params=pltpu.CompilerParams(vmem_limit_bytes=2**20),
    )(*[pltpu.with_memory_space_constraint(x, pltpu.VMEM) for x in results])


def solution(mesh):
    placed = P("seq", "head")
    return jax.shard_map(
        per_device,
        mesh=mesh,
        in_specs=(
            placed,
            placed,
            placed,
            placed,
            placed,
            P("seq"),
            P(),
            P("head", None),
            P("head"),
        ),
        out_specs=(placed,) * 5,
        check_vma=False,
    )
```

```python
import functools

import jax
import jax.numpy as jnp
from jax import lax
from jax.experimental import pallas as pl
from jax.experimental.pallas import tpu as pltpu
from jax.sharding import PartitionSpec as P

norm_eps = 1e-05
f32 = jnp.float32
bf16 = jnp.bfloat16
MESH = pl.DeviceIdType.MESH


def mm(a, b):
    return lax.dot_general(a, b, (((1,), (0,)), ((), ())), preferred_element_type=f32)


def mm_nt(a, b):
    return lax.dot_general(a, b, (((1,), (1,)), ((), ())), preferred_element_type=f32)


def kernel(
    groups,
    head_devices,
    offsets,
    q_in,
    k_in,
    v_in,
    gate_in,
    cot_in,
    gaps_in,
    lists_in,
    table_in,
    gain_in,
    layer_ref,
    dq_ref,
    dk_ref,
    dv_ref,
    dgate_ref,
    gate_ref,
    cot_ref,
    gaps_ref,
    gain_ref,
    lists_ref,
    table_ref,
    qbuf,
    kbuf,
    vbuf,
    gabuf,
    gprev,
    glater,
    sums_out,
    sums_in,
    slope_q,
    slope_k,
    weight_k,
    att_acc,
    dq_acc,
    dk_acc,
    dv_acc,
    local_sem,
    gap_send,
    gap_recv,
    q_send,
    q_recv,
    kv_send,
    kv_recv,
    sum_send,
    sum_recv,
    ga_send,
    ga_recv,
):
    rows, feats = q_in.shape
    heads, buckets = table_in.shape
    head_dim = feats // heads
    scaling = head_dim**-0.5
    full_width = feats * head_devices
    reach = offsets[-1]
    count = len(offsets)
    me = lax.axis_index("seq")
    head = lax.axis_index("head")

    def to_later(d, body):
        pl.when(me + d < groups)(body)

    def to_earlier(d, body):
        pl.when(me >= d)(body)

    pairs = (
        (k_in, kbuf.at[0]),
        (v_in, vbuf.at[0]),
        (gaps_in, gaps_ref),
        (table_in, table_ref),
        (lists_in, lists_ref),
        (gain_in, gain_ref),
        (q_in, qbuf.at[0]),
        (gate_in, gate_ref),
        (cot_in, cot_ref),
    )
    own = [pltpu.make_async_copy(src, dst, local_sem.at[i]) for i, (src, dst) in enumerate(pairs)]
    for copy in own:
        copy.start()

    barrier = pltpu.get_barrier_semaphore()

    def greet(axis, where):
        pl.semaphore_signal(barrier, inc=1, device_id={axis: where}, device_id_type=MESH)

    for k in range(1, reach + 1):
        to_later(k, lambda k=k: greet("seq", me + k))
        to_earlier(k, lambda k=k: greet("seq", me - k))
    for r in range(1, head_devices):
        greet("head", lax.rem(head + r, head_devices))
    pl.semaphore_wait(
        barrier,
        jnp.minimum(me, reach) + jnp.minimum(groups - 1 - me, reach) + head_devices - 1,
    )

    other_group = lax.rem(me + 1, groups)

    def remote(src, dst, send, recv, axis, where):
        return pltpu.make_async_remote_copy(
            src_ref=src,
            dst_ref=dst,
            send_sem=send,
            recv_sem=recv,
            device_id={axis: where},
            device_id_type=MESH,
        )

    def gaps_up(k):
        return remote(
            gaps_in, gprev.at[k - 1], gap_send.at[0, k - 1], gap_recv.at[0, k - 1], "seq", me + k
        )

    def gaps_down(k):
        return remote(
            gaps_in, glater.at[k - 1], gap_send.at[1, k - 1], gap_recv.at[1, k - 1], "seq", me - k
        )

    def block_copy(buf, which, source, s, where):
        return remote(
            buf.at[source],
            buf.at[s + 1],
            kv_send.at[which, s],
            kv_recv.at[which, s],
            "seq",
            where,
        )

    def pass_up(which, source, s, where):
        block_copy((kbuf, vbuf)[which], which, source, s, where).start()

    def first_up(which):
        near = (me % 2 == 0) & (me + 1 < groups)
        if count > 1:
            pl.when(me + 2 < groups)(lambda: pass_up(which, 0, 1, me + 2))
        pl.when(near)(lambda: pass_up(which, 0, 0, me + 1))

    def relay_up(which, s):
        if s == 1:
            pl.when((me % 2 == 1) & (me >= 2))(lambda: pass_up(which, 2, 0, me - 1))
        if 1 <= s < count - 1:
            step = offsets[s]
            pl.when((me >= step) & (me + step < groups))(
                lambda: pass_up(which, s + 1, s + 1, me + step)
            )

    def wait_block(which, s):
        block_copy((kbuf, vbuf)[which], which, 0, s, other_group).wait_recv()

    def wait_block_sent(which, s):
        block_copy((kbuf, vbuf)[which], which, 0, s, other_group).wait_send()

    def queries_down(s):
        return remote(q_in, qbuf.at[s + 1], q_send.at[s], q_recv.at[s], "seq", me - offsets[s])

    def grads_down(s):
        return remote(
            gabuf.at[0], gabuf.at[s + 1], ga_send.at[s], ga_recv.at[s], "seq", me - offsets[s]
        )

    def sums_to(r):
        return remote(
            sums_out,
            sums_in.at[r - 1],
            sum_send.at[r - 1],
            sum_recv.at[r - 1],
            "head",
            lax.rem(head + r, head_devices),
        )

    for k in range(1, reach + 1):
        to_later(k, lambda k=k: gaps_up(k).start())
        to_earlier(k, lambda k=k: gaps_down(k).start())
    own[0].wait()
    own[1].wait()
    first_up(0)
    first_up(1)
    for s in range(count):
        to_earlier(offsets[s], lambda s=s: queries_down(s).start())

    for k in range(1, reach + 1):

        def no_earlier(k=k):
            gprev[k - 1] = jnp.zeros_like(gprev[k - 1])

        def no_later(k=k):
            glater[k - 1] = jnp.zeros_like(glater[k - 1])

        pl.when(me < k)(no_earlier)
        pl.when(me + k >= groups)(no_later)

    row_ids = lax.broadcasted_iota(jnp.int32, (rows, rows), 0)
    col_ids = lax.broadcasted_iota(jnp.int32, (rows, rows), 1)
    upper = (row_ids <= col_ids).astype(f32)
    upper_bf = upper.astype(bf16)
    ones = jnp.ones((rows, rows), bf16)
    lane_head = lax.broadcasted_iota(jnp.int32, (rows, feats), 1) // head_dim
    sub_head = lax.broadcasted_iota(jnp.int32, (feats, rows), 0) // head_dim
    lane_masks = [(lane_head == h).astype(bf16) for h in range(heads)]
    sub_masks = [(sub_head == h).astype(bf16) for h in range(heads)]

    def prefix_row(gaps):
        wide = jnp.broadcast_to(gaps, (8, rows)).astype(bf16)
        return mm(wide, upper_bf)[0:1]

    def after_column(gaps):
        return mm(jnp.where(col_ids > row_ids, gaps, 0.0).astype(bf16), ones)

    def bias(delta):
        parts = [jnp.full(delta.shape, table_ref[h, 0], f32) for h in range(heads)]
        for b in range(1, buckets):
            reached = delta >= float(2 ** (b - 1))
            parts = [jnp.where(reached, table_ref[h, b], parts[h]) for h in range(heads)]
        return jnp.concatenate(parts, axis=1)

    def by_head_rows(q):
        return jnp.concatenate([q * mask for mask in lane_masks], axis=0)

    def by_head_lanes(g):
        return jnp.concatenate([g * mask for mask in sub_masks], axis=1)

    def own_heads(wide):
        return jnp.concatenate(
            [
                wide[h * head_dim : (h + 1) * head_dim, h * rows : (h + 1) * rows]
                for h in range(heads)
            ],
            axis=0,
        )

    def activate(keys, queries, biases, mask):
        scores = mm_nt(keys, queries) * scaling + biases
        sig = 0.5 * jnp.tanh(0.5 * scores) + 0.5
        weights = scores * sig
        slope = sig + weights * (1.0 - sig)
        return (weights * mask).astype(bf16), slope * mask

    for copy in own[2:]:
        copy.wait()
    own_gaps = gaps_ref[...].astype(f32)
    own_total = jnp.sum(own_gaps, axis=1, keepdims=True)
    own_row = prefix_row(own_gaps)
    own_after = after_column(own_gaps)
    diag_bias = bias(own_row + own_after - own_total)
    diag_mask = jnp.concatenate([upper] * heads, axis=1)
    gain = gain_ref[...]
    gates = gate_ref[...].astype(f32)
    upstream = cot_ref[...].astype(f32)
    scaled = (upstream * gates * gain).T

    keys = kbuf[0]
    values = vbuf[0]
    queries = by_head_rows(qbuf[0])
    diag_weights, diag_slope = activate(keys, queries, diag_bias, diag_mask)
    att_acc[...] = mm(values.T, diag_weights)

    def receive(s):
        for which in range(2):

            def arrived(which=which):
                wait_block(which, s)
                relay_up(which, s)

            to_earlier(offsets[s], arrived)

    for k in range(1, reach + 1):
        to_earlier(k, lambda k=k: gaps_up(k).wait_recv())
        to_later(k, lambda k=k: gaps_down(k).wait_recv())

    def between(buf, d):
        if d == 1:
            return jnp.zeros((1, 1), f32)
        return jnp.sum(
            jnp.sum(buf[0 : d - 1].astype(f32), axis=0), axis=1, keepdims=True
        )

    biases = []
    for s, d in enumerate(offsets):
        after = after_column(gprev[d - 1].astype(f32))
        biases.append(bias(own_row + after + between(gprev, d)))
    if count > 1:
        receive(1)

    for s, d in enumerate(offsets):

        def score_later(s=s, d=d):
            row = prefix_row(glater[d - 1].astype(f32))
            later_bias = bias(row + own_after + between(glater, d))
            listed = (lists_ref[me + d, s] >= 0).astype(f32)
            queries_down(s).wait_recv()
            weights, slope = activate(keys, by_head_rows(qbuf[s + 1]), later_bias, listed)
            weight_k[s] = weights
            slope_k[s] = slope

        to_later(d, score_later)

    order = [s for s in (1, 0) if s < count] + list(range(2, count))
    for s in order:
        d = offsets[s]
        if s != 1:
            receive(s)

        def attend(s=s):
            listed = (lists_ref[me, s] >= 0).astype(f32)
            weights, slope = activate(kbuf[s + 1], queries, biases[s], listed)
            slope_q[s] = slope
            att_acc[...] += mm(vbuf[s + 1].T, weights)

        to_earlier(d, attend)

    flat = own_heads(att_acc[...])
    own_sums = [
        jnp.sum(x, axis=0, keepdims=True) for x in (flat, flat * flat, scaled, scaled * flat)
    ]
    sums_out[...] = jnp.concatenate(own_sums + [jnp.zeros((4, rows), f32)], axis=0)
    for r in range(1, head_devices):
        sums_to(r).start()

    for r in range(1, head_devices):
        sums_to(r).wait_recv()
    sums = sums_out[...]
    for r in range(1, head_devices):
        sums = sums + sums_in[r - 1]
    mean = sums[0:1] / full_width
    var = sums[1:2] / full_width - mean * mean
    inv_std = lax.rsqrt(var + norm_eps)
    centered = (flat - mean) * inv_std
    scaled_mean = sums[2:3] / full_width
    product_mean = inv_std * (sums[3:4] - mean * sums[2:3]) / full_width
    grad = (inv_std * (scaled - scaled_mean - centered * product_mean)).astype(bf16)
    gabuf[0] = grad
    for s in range(count):
        to_earlier(offsets[s], lambda s=s: grads_down(s).start())

    grads = by_head_lanes(grad)
    diag_grad = (mm(values, grads) * diag_slope).astype(bf16)
    dq_acc[...] = mm(keys.T, diag_grad)
    dk_acc[...] = mm(diag_grad, queries)
    dv_acc[...] = mm_nt(diag_weights, grads)
    for s, d in enumerate(offsets):

        def query_part(s=s):
            grad_scores = (mm(vbuf[s + 1], grads) * slope_q[s]).astype(bf16)
            dq_acc[...] += mm(kbuf[s + 1].T, grad_scores)

        to_earlier(d, query_part)
    dq_ref[...] = (own_heads(dq_acc[...]) * scaling).T.astype(bf16)
    normed = centered.T * gain
    layer_ref[...] = (normed * gates).astype(bf16)
    dgate_ref[...] = (upstream * normed).astype(bf16)

    for s, d in enumerate(offsets):

        def key_part(s=s):
            grads_down(s).wait_recv()
            grads = by_head_lanes(gabuf[s + 1])
            grad_scores = (mm(values, grads) * slope_k[s]).astype(bf16)
            dk_acc[...] += mm(grad_scores, by_head_rows(qbuf[s + 1]))
            dv_acc[...] += mm_nt(weight_k[s], grads)

        to_later(d, key_part)
    dk_ref[...] = (dk_acc[...] * scaling).astype(bf16)
    dv_ref[...] = dv_acc[...].astype(bf16)

    for k in range(1, reach + 1):
        to_later(k, lambda k=k: gaps_up(k).wait_send())
        to_earlier(k, lambda k=k: gaps_down(k).wait_send())
    for s, d in enumerate(offsets):
        if s == 0:
            sent_up = ((me % 2 == 0) & (me + 1 < groups)) | ((me % 2 == 1) & (me >= 2))
        elif s == 1:
            sent_up = me + 2 < groups
        else:
            sent_up = (me >= d // 2) & (me + d // 2 < groups)
        for which in range(2):
            pl.when(sent_up)(lambda which=which, s=s: wait_block_sent(which, s))
        to_earlier(d, lambda s=s: queries_down(s).wait_send())
        to_earlier(d, lambda s=s: grads_down(s).wait_send())
    for r in range(1, head_devices):
        sums_to(r).wait_send()


def hand_out(*refs):
    sems = refs[-1]
    copies = [pltpu.make_async_copy(refs[i], refs[i + 5], sems.at[i]) for i in range(5)]
    for copy in copies:
        copy.start()
    for copy in copies:
        copy.wait()


def per_device(
    query_rows,
    key_rows,
    value_rows,
    gate_rows,
    cotangent,
    event_gaps,
    block_lists,
    bias_table,
    norm_gain,
):
    rows, feats = query_rows.shape
    heads = bias_table.shape[0]
    groups = lax.axis_size("seq")
    head_devices = lax.axis_size("head")
    offsets = [2**s for s in range(block_lists.shape[1]) if 2**s < groups]
    count = len(offsets)
    reach = offsets[-1]
    hbm = pl.BlockSpec(memory_space=pltpu.HBM)
    vmem = pl.BlockSpec(memory_space=pltpu.VMEM)
    dma = pltpu.SemaphoreType.DMA
    operands = (
        query_rows,
        key_rows,
        value_rows,
        gate_rows,
        cotangent,
        event_gaps.reshape(1, rows),
        block_lists,
        bias_table,
        norm_gain.reshape(1, feats),
    )
    results = pl.pallas_call(
        functools.partial(kernel, groups, head_devices, offsets),
        out_shape=[pltpu.VMEM((rows, feats), bf16)] * 5,
        in_specs=[hbm] * 9,
        out_specs=[vmem] * 5,
        scratch_shapes=[
            pltpu.VMEM((rows, feats), bf16),
            pltpu.VMEM((rows, feats), bf16),
            pltpu.VMEM((1, rows), jnp.int32),
            pltpu.VMEM((1, feats), f32),
            pltpu.SMEM(block_lists.shape, jnp.int32),
            pltpu.SMEM(bias_table.shape, f32),
            pltpu.VMEM((count + 1, rows, feats), bf16),
            pltpu.VMEM((count + 1, rows, feats), bf16),
            pltpu.VMEM((count + 1, rows, feats), bf16),
            pltpu.VMEM((count + 1, feats, rows), bf16),
            pltpu.VMEM((reach, 1, rows), jnp.int32),
            pltpu.VMEM((reach, 1, rows), jnp.int32),
            pltpu.VMEM((8, rows), f32),
            pltpu.VMEM((head_devices - 1, 8, rows), f32),
            pltpu.VMEM((count, rows, heads * rows), f32),
            pltpu.VMEM((count, rows, heads * rows), f32),
            pltpu.VMEM((count, rows, heads * rows), bf16),
            pltpu.VMEM((feats, heads * rows), f32),
            pltpu.VMEM((feats, heads * rows), f32),
            pltpu.VMEM((rows, feats), f32),
            pltpu.VMEM((rows, feats), f32),
            dma((9,)),
            dma((2, reach)),
            dma((2, reach)),
            dma((count,)),
            dma((count,)),
            dma((2, count)),
            dma((2, count)),
            dma((head_devices - 1,)),
            dma((head_devices - 1,)),
            dma((count,)),
            dma((count,)),
        ],
        compiler_params=pltpu.CompilerParams(
            collective_id=0, has_side_effects=True, vmem_limit_bytes=24 * 2**20
        ),
    )(*[pltpu.with_memory_space_constraint(x, pltpu.HBM) for x in operands])
    return pl.pallas_call(
        hand_out,
        out_shape=[jax.ShapeDtypeStruct((rows, feats), bf16)] * 5,
        in_specs=[vmem] * 5,
        out_specs=[hbm] * 5,
        scratch_shapes=[dma((5,))],
        compiler_params=pltpu.CompilerParams(vmem_limit_bytes=2**20),
    )(*[pltpu.with_memory_space_constraint(x, pltpu.VMEM) for x in results])


def solution(mesh):
    placed = P("seq", "head")
    return jax.shard_map(
        per_device,
        mesh=mesh,
        in_specs=(
            placed,
            placed,
            placed,
            placed,
            placed,
            P("seq"),
            P(),
            P("head", None),
            P("head"),
        ),
        out_specs=(placed,) * 5,
        check_vma=False,
    )
```

```python
import functools

import jax
import jax.numpy as jnp
from jax import lax
from jax.experimental import pallas as pl
from jax.experimental.pallas import tpu as pltpu
from jax.sharding import PartitionSpec as P

norm_eps = 1e-05
f32 = jnp.float32
bf16 = jnp.bfloat16
MESH = pl.DeviceIdType.MESH


def mm(a, b):
    return lax.dot_general(a, b, (((1,), (0,)), ((), ())), preferred_element_type=f32)


def mm_nt(a, b):
    return lax.dot_general(a, b, (((1,), (1,)), ((), ())), preferred_element_type=f32)


def kernel(
    groups,
    head_devices,
    offsets,
    q_in,
    k_in,
    v_in,
    gate_in,
    cot_in,
    gaps_in,
    lists_in,
    table_in,
    gain_in,
    layer_ref,
    dq_ref,
    dk_ref,
    dv_ref,
    dgate_ref,
    gate_ref,
    cot_ref,
    gaps_ref,
    gain_ref,
    lists_ref,
    table_ref,
    qbuf,
    kbuf,
    vbuf,
    gabuf,
    gprev,
    glater,
    sums_out,
    sums_in,
    slope_q,
    slope_k,
    weight_k,
    local_sem,
    gap_send,
    gap_recv,
    q_send,
    q_recv,
    kv_send,
    kv_recv,
    sum_send,
    sum_recv,
    ga_send,
    ga_recv,
):
    rows, feats = q_in.shape
    heads, buckets = table_in.shape
    head_dim = feats // heads
    scaling = head_dim**-0.5
    full_width = feats * head_devices
    reach = offsets[-1]
    count = len(offsets)
    me = lax.axis_index("seq")
    head = lax.axis_index("head")

    def to_later(d, body):
        pl.when(me + d < groups)(body)

    def to_earlier(d, body):
        pl.when(me >= d)(body)

    pairs = (
        (gaps_in, gaps_ref),
        (table_in, table_ref),
        (lists_in, lists_ref),
        (gain_in, gain_ref),
        (k_in, kbuf.at[0]),
        (q_in, qbuf.at[0]),
        (v_in, vbuf.at[0]),
        (gate_in, gate_ref),
        (cot_in, cot_ref),
    )
    own = [pltpu.make_async_copy(src, dst, local_sem.at[i]) for i, (src, dst) in enumerate(pairs)]
    for copy in own:
        copy.start()

    barrier = pltpu.get_barrier_semaphore()

    def greet(axis, where):
        pl.semaphore_signal(barrier, inc=1, device_id={axis: where}, device_id_type=MESH)

    for k in range(1, reach + 1):
        to_later(k, lambda k=k: greet("seq", me + k))
        to_earlier(k, lambda k=k: greet("seq", me - k))
    for r in range(1, head_devices):
        greet("head", lax.rem(head + r, head_devices))
    pl.semaphore_wait(
        barrier,
        jnp.minimum(me, reach) + jnp.minimum(groups - 1 - me, reach) + head_devices - 1,
    )

    def remote(src, dst, send, recv, axis, where):
        return pltpu.make_async_remote_copy(
            src_ref=src,
            dst_ref=dst,
            send_sem=send,
            recv_sem=recv,
            device_id={axis: where},
            device_id_type=MESH,
        )

    def gaps_up(k):
        return remote(
            gaps_in, gprev.at[k - 1], gap_send.at[0, k - 1], gap_recv.at[0, k - 1], "seq", me + k
        )

    def gaps_down(k):
        return remote(
            gaps_in, glater.at[k - 1], gap_send.at[1, k - 1], gap_recv.at[1, k - 1], "seq", me - k
        )

    def keys_up(s):
        return remote(
            k_in, kbuf.at[s + 1], kv_send.at[0, s], kv_recv.at[0, s], "seq", me + offsets[s]
        )

    def values_up(s):
        return remote(
            v_in, vbuf.at[s + 1], kv_send.at[1, s], kv_recv.at[1, s], "seq", me + offsets[s]
        )

    def queries_down(s):
        return remote(q_in, qbuf.at[s + 1], q_send.at[s], q_recv.at[s], "seq", me - offsets[s])

    def grads_down(s):
        return remote(
            gabuf.at[0], gabuf.at[s + 1], ga_send.at[s], ga_recv.at[s], "seq", me - offsets[s]
        )

    def sums_to(r):
        return remote(
            sums_out,
            sums_in.at[r - 1],
            sum_send.at[r - 1],
            sum_recv.at[r - 1],
            "head",
            lax.rem(head + r, head_devices),
        )

    for k in range(1, reach + 1):
        to_later(k, lambda k=k: gaps_up(k).start())
        to_earlier(k, lambda k=k: gaps_down(k).start())
    for s in range(count):
        to_later(offsets[s], lambda s=s: keys_up(s).start())
        to_later(offsets[s], lambda s=s: values_up(s).start())
        to_earlier(offsets[s], lambda s=s: queries_down(s).start())

    for k in range(1, reach + 1):

        def no_earlier(k=k):
            gprev[k - 1] = jnp.zeros_like(gprev[k - 1])

        def no_later(k=k):
            glater[k - 1] = jnp.zeros_like(glater[k - 1])

        pl.when(me < k)(no_earlier)
        pl.when(me + k >= groups)(no_later)
    for s, d in enumerate(offsets):

        def no_keys(s=s):
            kbuf[s + 1] = jnp.zeros((rows, feats), bf16)
            vbuf[s + 1] = jnp.zeros((rows, feats), bf16)

        def no_queries(s=s):
            qbuf[s + 1] = jnp.zeros((rows, feats), bf16)
            gabuf[s + 1] = jnp.zeros((feats, rows), bf16)

        pl.when(me < d)(no_keys)
        pl.when(me + d >= groups)(no_queries)

    row_ids = lax.broadcasted_iota(jnp.int32, (rows, rows), 0)
    col_ids = lax.broadcasted_iota(jnp.int32, (rows, rows), 1)
    upper = (row_ids <= col_ids).astype(f32)
    upper_bf = upper.astype(bf16)
    ones = jnp.ones((rows, rows), bf16)
    lane_head = lax.broadcasted_iota(jnp.int32, (rows, feats), 1) // head_dim
    sub_head = lax.broadcasted_iota(jnp.int32, (feats, rows), 0) // head_dim
    lane_masks = [(lane_head == h).astype(bf16) for h in range(heads)]
    sub_masks = [(sub_head == h).astype(bf16) for h in range(heads)]

    def prefix_row(gaps):
        wide = jnp.broadcast_to(gaps, (8, rows)).astype(bf16)
        return mm(wide, upper_bf)[0:1]

    def after_column(gaps):
        return mm(jnp.where(col_ids > row_ids, gaps, 0.0).astype(bf16), ones)

    def bias(delta):
        whole = jnp.maximum(delta, 0.0).astype(jnp.int32)
        bucket = jnp.minimum(32 - lax.clz(whole), buckets - 1)
        return jnp.concatenate(
            [jnp.take_along_axis(table, bucket, axis=1) for table in tables], axis=1
        )

    def by_head_rows(q):
        return jnp.concatenate([q * mask for mask in lane_masks], axis=0)

    def by_head_lanes(g):
        return jnp.concatenate([g * mask for mask in sub_masks], axis=1)

    def own_heads(wide):
        return jnp.concatenate(
            [
                wide[h * head_dim : (h + 1) * head_dim, h * rows : (h + 1) * rows]
                for h in range(heads)
            ],
            axis=0,
        )

    def activate(products, biases, mask):
        scores = products * scaling + biases
        sig = 0.5 * jnp.tanh(0.5 * scores) + 0.5
        weights = scores * sig
        slope = sig + weights * (1.0 - sig)
        return (weights * mask).astype(bf16), slope * mask

    for copy in own:
        copy.wait()
    lanes = lax.broadcasted_iota(jnp.int32, (rows, rows), 1)
    tables = []
    for h in range(heads):
        table = jnp.zeros((rows, rows), f32)
        for b in range(buckets):
            table = jnp.where(lanes == b, table_ref[h, b], table)
        tables.append(table)
    own_gaps = gaps_ref[...].astype(f32)
    own_total = jnp.sum(own_gaps, axis=1, keepdims=True)
    own_row = prefix_row(own_gaps)
    own_after = after_column(own_gaps)
    diag_bias = bias(own_row + own_after - own_total)
    diag_mask = jnp.concatenate([upper] * heads, axis=1)
    gain = gain_ref[...]
    gates = gate_ref[...].astype(f32)
    upstream = cot_ref[...].astype(f32)
    scaled = (upstream * gates * gain).T

    keys = kbuf[0]
    values = vbuf[0]
    queries = by_head_rows(qbuf[0])
    diag_weights, diag_slope = activate(mm_nt(keys, queries), diag_bias, diag_mask)
    attended = mm(values.T, diag_weights)

    for k in range(1, reach + 1):
        to_earlier(k, lambda k=k: gaps_up(k).wait_recv())
        to_later(k, lambda k=k: gaps_down(k).wait_recv())

    def between(buf, d):
        if d == 1:
            return jnp.zeros((1, 1), f32)
        return jnp.sum(
            jnp.sum(buf[0 : d - 1].astype(f32), axis=0), axis=1, keepdims=True
        )

    biases = []
    for s, d in enumerate(offsets):
        after = after_column(gprev[d - 1].astype(f32))
        biases.append(bias(own_row + after + between(gprev, d)))
    for s, d in enumerate(offsets):
        to_earlier(d, lambda s=s: keys_up(s).wait_recv())
        to_earlier(d, lambda s=s: values_up(s).wait_recv())
    early_keys = kbuf[1 : count + 1].reshape(count * rows, feats)
    early_values = vbuf[1 : count + 1].reshape(count * rows, feats)
    early_scores = mm_nt(early_keys, queries)
    early_weights = []
    for s in range(count):
        listed = (lists_ref[me, s] >= 0).astype(f32)
        part = early_scores[s * rows : (s + 1) * rows]
        weights, slope = activate(part, biases[s], listed)
        slope_q[s] = slope
        early_weights.append(weights)
    attended = attended + mm(early_values.T, jnp.concatenate(early_weights, axis=0))

    flat = own_heads(attended)
    own_sums = [
        jnp.sum(x, axis=0, keepdims=True) for x in (flat, flat * flat, scaled, scaled * flat)
    ]
    sums_out[...] = jnp.concatenate(own_sums + [jnp.zeros((4, rows), f32)], axis=0)
    for r in range(1, head_devices):
        sums_to(r).start()

    for s, d in enumerate(offsets):
        to_later(d, lambda s=s: queries_down(s).wait_recv())
    late_queries = jnp.concatenate([by_head_rows(qbuf[s + 1]) for s in range(count)], axis=0)
    late_scores = mm_nt(keys, late_queries)
    wide = heads * rows
    for s, d in enumerate(offsets):
        row = prefix_row(glater[d - 1].astype(f32))
        later_bias = bias(row + own_after + between(glater, d))
        there = jnp.minimum(me + d, groups - 1)
        listed = ((lists_ref[there, s] >= 0) & (me + d < groups)).astype(f32)
        part = late_scores[:, s * wide : (s + 1) * wide]
        weights, slope = activate(part, later_bias, listed)
        weight_k[:, s * wide : (s + 1) * wide] = weights
        slope_k[:, s * wide : (s + 1) * wide] = slope

    for r in range(1, head_devices):
        sums_to(r).wait_recv()
    sums = sums_out[...]
    for r in range(1, head_devices):
        sums = sums + sums_in[r - 1]
    mean = sums[0:1] / full_width
    var = sums[1:2] / full_width - mean * mean
    inv_std = lax.rsqrt(var + norm_eps)
    centered = (flat - mean) * inv_std
    scaled_mean = sums[2:3] / full_width
    product_mean = inv_std * (sums[3:4] - mean * sums[2:3]) / full_width
    grad = (inv_std * (scaled - scaled_mean - centered * product_mean)).astype(bf16)
    gabuf[0] = grad
    for s in range(count):
        to_earlier(offsets[s], lambda s=s: grads_down(s).start())

    grads = by_head_lanes(grad)
    diag_grad = (mm(values, grads) * diag_slope).astype(bf16)
    early_products = mm(early_values, grads)
    grad_scores = jnp.concatenate(
        [
            (early_products[s * rows : (s + 1) * rows] * slope_q[s]).astype(bf16)
            for s in range(count)
        ],
        axis=0,
    )
    dq = mm(keys.T, diag_grad) + mm(early_keys.T, grad_scores)
    dk = mm(diag_grad, queries)
    dv = mm_nt(diag_weights, grads)
    dq_ref[...] = (own_heads(dq) * scaling).T.astype(bf16)
    normed = centered.T * gain
    layer_ref[...] = (normed * gates).astype(bf16)
    dgate_ref[...] = (upstream * normed).astype(bf16)

    for s, d in enumerate(offsets):
        to_later(d, lambda s=s: grads_down(s).wait_recv())
    late_grads = jnp.concatenate([by_head_lanes(gabuf[s + 1]) for s in range(count)], axis=1)
    late_products = (mm(values, late_grads) * slope_k[...]).astype(bf16)
    dk = dk + mm(late_products, late_queries)
    dv = dv + mm_nt(weight_k[...], late_grads)
    dk_ref[...] = (dk * scaling).astype(bf16)
    dv_ref[...] = dv.astype(bf16)

    for k in range(1, reach + 1):
        to_later(k, lambda k=k: gaps_up(k).wait_send())
        to_earlier(k, lambda k=k: gaps_down(k).wait_send())
    for s, d in enumerate(offsets):
        to_later(d, lambda s=s: keys_up(s).wait_send())
        to_later(d, lambda s=s: values_up(s).wait_send())
        to_earlier(d, lambda s=s: queries_down(s).wait_send())
        to_earlier(d, lambda s=s: grads_down(s).wait_send())
    for r in range(1, head_devices):
        sums_to(r).wait_send()


def hand_out(*refs):
    sems = refs[-1]
    copies = [pltpu.make_async_copy(refs[i], refs[i + 5], sems.at[i]) for i in range(5)]
    for copy in copies:
        copy.start()
    for copy in copies:
        copy.wait()


def per_device(
    query_rows,
    key_rows,
    value_rows,
    gate_rows,
    cotangent,
    event_gaps,
    block_lists,
    bias_table,
    norm_gain,
):
    rows, feats = query_rows.shape
    heads = bias_table.shape[0]
    groups = lax.axis_size("seq")
    head_devices = lax.axis_size("head")
    offsets = [2**s for s in range(block_lists.shape[1]) if 2**s < groups]
    count = len(offsets)
    reach = offsets[-1]
    hbm = pl.BlockSpec(memory_space=pltpu.HBM)
    vmem = pl.BlockSpec(memory_space=pltpu.VMEM)
    dma = pltpu.SemaphoreType.DMA
    operands = (
        query_rows,
        key_rows,
        value_rows,
        gate_rows,
        cotangent,
        event_gaps.reshape(1, rows),
        block_lists,
        bias_table,
        norm_gain.reshape(1, feats),
    )
    results = pl.pallas_call(
        functools.partial(kernel, groups, head_devices, offsets),
        out_shape=[pltpu.VMEM((rows, feats), bf16)] * 5,
        in_specs=[hbm] * 9,
        out_specs=[vmem] * 5,
        scratch_shapes=[
            pltpu.VMEM((rows, feats), bf16),
            pltpu.VMEM((rows, feats), bf16),
            pltpu.VMEM((1, rows), jnp.int32),
            pltpu.VMEM((1, feats), f32),
            pltpu.SMEM(block_lists.shape, jnp.int32),
            pltpu.SMEM(bias_table.shape, f32),
            pltpu.VMEM((count + 1, rows, feats), bf16),
            pltpu.VMEM((count + 1, rows, feats), bf16),
            pltpu.VMEM((count + 1, rows, feats), bf16),
            pltpu.VMEM((count + 1, feats, rows), bf16),
            pltpu.VMEM((reach, 1, rows), jnp.int32),
            pltpu.VMEM((reach, 1, rows), jnp.int32),
            pltpu.VMEM((8, rows), f32),
            pltpu.VMEM((head_devices - 1, 8, rows), f32),
            pltpu.VMEM((count, rows, heads * rows), f32),
            pltpu.VMEM((rows, count * heads * rows), f32),
            pltpu.VMEM((rows, count * heads * rows), bf16),
            dma((9,)),
            dma((2, reach)),
            dma((2, reach)),
            dma((count,)),
            dma((count,)),
            dma((2, count)),
            dma((2, count)),
            dma((head_devices - 1,)),
            dma((head_devices - 1,)),
            dma((count,)),
            dma((count,)),
        ],
        compiler_params=pltpu.CompilerParams(
            collective_id=0, has_side_effects=True, vmem_limit_bytes=24 * 2**20
        ),
    )(*[pltpu.with_memory_space_constraint(x, pltpu.HBM) for x in operands])
    return pl.pallas_call(
        hand_out,
        out_shape=[jax.ShapeDtypeStruct((rows, feats), bf16)] * 5,
        in_specs=[vmem] * 5,
        out_specs=[hbm] * 5,
        scratch_shapes=[dma((5,))],
        compiler_params=pltpu.CompilerParams(vmem_limit_bytes=2**20),
    )(*[pltpu.with_memory_space_constraint(x, pltpu.VMEM) for x in results])


def solution(mesh):
    placed = P("seq", "head")
    return jax.shard_map(
        per_device,
        mesh=mesh,
        in_specs=(
            placed,
            placed,
            placed,
            placed,
            placed,
            P("seq"),
            P(),
            P("head", None),
            P("head"),
        ),
        out_specs=(placed,) * 5,
        check_vma=False,
    )
```

```python
import functools

import jax
import jax.numpy as jnp
from jax import lax
from jax.experimental import pallas as pl
from jax.experimental.pallas import tpu as pltpu
from jax.sharding import PartitionSpec as P

norm_eps = 1e-05
f32 = jnp.float32
bf16 = jnp.bfloat16
MESH = pl.DeviceIdType.MESH


def mm(a, b):
    return lax.dot_general(a, b, (((1,), (0,)), ((), ())), preferred_element_type=f32)


def mm_nt(a, b):
    return lax.dot_general(a, b, (((1,), (1,)), ((), ())), preferred_element_type=f32)


def kernel(
    groups,
    head_devices,
    offsets,
    q_in,
    k_in,
    v_in,
    gate_in,
    cot_in,
    gaps_in,
    lists_in,
    table_in,
    gain_in,
    layer_ref,
    dq_ref,
    dk_ref,
    dv_ref,
    dgate_ref,
    gate_ref,
    cot_ref,
    gaps_ref,
    gain_ref,
    lists_ref,
    table_ref,
    qbuf,
    kbuf,
    vbuf,
    gabuf,
    gprev,
    glater,
    sums_out,
    sums_in,
    slope_q,
    slope_k,
    weight_k,
    local_sem,
    gap_send,
    gap_recv,
    q_send,
    q_recv,
    kv_send,
    kv_recv,
    sum_send,
    sum_recv,
    ga_send,
    ga_recv,
):
    rows, feats = q_in.shape
    heads, buckets = table_in.shape
    head_dim = feats // heads
    scaling = head_dim**-0.5
    full_width = feats * head_devices
    reach = offsets[-1]
    count = len(offsets)
    me = lax.axis_index("seq")
    head = lax.axis_index("head")

    def to_later(d, body):
        pl.when(me + d < groups)(body)

    def to_earlier(d, body):
        pl.when(me >= d)(body)

    pairs = (
        (k_in, kbuf.at[0]),
        (v_in, vbuf.at[0]),
        (gaps_in, gaps_ref),
        (table_in, table_ref),
        (lists_in, lists_ref),
        (gain_in, gain_ref),
        (q_in, qbuf.at[0]),
        (gate_in, gate_ref),
        (cot_in, cot_ref),
    )
    own = [pltpu.make_async_copy(src, dst, local_sem.at[i]) for i, (src, dst) in enumerate(pairs)]
    for copy in own:
        copy.start()

    barrier = pltpu.get_barrier_semaphore()

    def greet(axis, where):
        pl.semaphore_signal(barrier, inc=1, device_id={axis: where}, device_id_type=MESH)

    for k in range(1, reach + 1):
        to_later(k, lambda k=k: greet("seq", me + k))
        to_earlier(k, lambda k=k: greet("seq", me - k))
    for r in range(1, head_devices):
        greet("head", lax.rem(head + r, head_devices))
    pl.semaphore_wait(
        barrier,
        jnp.minimum(me, reach) + jnp.minimum(groups - 1 - me, reach) + head_devices - 1,
    )

    other_group = lax.rem(me + 1, groups)

    def remote(src, dst, send, recv, axis, where):
        return pltpu.make_async_remote_copy(
            src_ref=src,
            dst_ref=dst,
            send_sem=send,
            recv_sem=recv,
            device_id={axis: where},
            device_id_type=MESH,
        )

    def gaps_up(k):
        return remote(
            gaps_in, gprev.at[k - 1], gap_send.at[0, k - 1], gap_recv.at[0, k - 1], "seq", me + k
        )

    def gaps_down(k):
        return remote(
            gaps_in, glater.at[k - 1], gap_send.at[1, k - 1], gap_recv.at[1, k - 1], "seq", me - k
        )

    def block_copy(buf, which, source, s, where):
        return remote(
            buf.at[source],
            buf.at[s + 1],
            kv_send.at[which, s],
            kv_recv.at[which, s],
            "seq",
            where,
        )

    def pass_up(which, source, s, where):
        block_copy((kbuf, vbuf)[which], which, source, s, where).start()

    def first_up(which):
        near = (me % 2 == 0) & (me + 1 < groups)
        if count > 1:
            pl.when(me + 2 < groups)(lambda: pass_up(which, 0, 1, me + 2))
        pl.when(near)(lambda: pass_up(which, 0, 0, me + 1))

    def relay_up(which, s):
        if s == 1:
            pl.when((me % 2 == 1) & (me >= 2))(lambda: pass_up(which, 2, 0, me - 1))
        if 1 <= s < count - 1:
            step = offsets[s]
            pl.when((me >= step) & (me + step < groups))(
                lambda: pass_up(which, s + 1, s + 1, me + step)
            )

    def wait_block(which, s):
        block_copy((kbuf, vbuf)[which], which, 0, s, other_group).wait_recv()

    def wait_block_sent(which, s):
        block_copy((kbuf, vbuf)[which], which, 0, s, other_group).wait_send()

    def queries_down(s):
        return remote(q_in, qbuf.at[s + 1], q_send.at[s], q_recv.at[s], "seq", me - offsets[s])

    def grads_down(s):
        return remote(
            gabuf.at[0], gabuf.at[s + 1], ga_send.at[s], ga_recv.at[s], "seq", me - offsets[s]
        )

    def sums_to(r):
        return remote(
            sums_out,
            sums_in.at[r - 1],
            sum_send.at[r - 1],
            sum_recv.at[r - 1],
            "head",
            lax.rem(head + r, head_devices),
        )

    for k in range(1, reach + 1):
        to_later(k, lambda k=k: gaps_up(k).start())
        to_earlier(k, lambda k=k: gaps_down(k).start())
    own[0].wait()
    own[1].wait()
    first_up(0)
    first_up(1)
    for s in range(count):
        to_earlier(offsets[s], lambda s=s: queries_down(s).start())

    for k in range(1, reach + 1):

        def no_earlier(k=k):
            gprev[k - 1] = jnp.zeros_like(gprev[k - 1])

        def no_later(k=k):
            glater[k - 1] = jnp.zeros_like(glater[k - 1])

        pl.when(me < k)(no_earlier)
        pl.when(me + k >= groups)(no_later)
    for s, d in enumerate(offsets):

        def no_keys(s=s):
            kbuf[s + 1] = jnp.zeros((rows, feats), bf16)
            vbuf[s + 1] = jnp.zeros((rows, feats), bf16)

        def no_queries(s=s):
            qbuf[s + 1] = jnp.zeros((rows, feats), bf16)
            gabuf[s + 1] = jnp.zeros((feats, rows), bf16)

        pl.when(me < d)(no_keys)
        pl.when(me + d >= groups)(no_queries)

    row_ids = lax.broadcasted_iota(jnp.int32, (rows, rows), 0)
    col_ids = lax.broadcasted_iota(jnp.int32, (rows, rows), 1)
    upper = (row_ids <= col_ids).astype(f32)
    upper_bf = upper.astype(bf16)
    ones = jnp.ones((rows, rows), bf16)
    lane_head = lax.broadcasted_iota(jnp.int32, (rows, feats), 1) // head_dim
    sub_head = lax.broadcasted_iota(jnp.int32, (feats, rows), 0) // head_dim
    lane_masks = [(lane_head == h).astype(bf16) for h in range(heads)]
    sub_masks = [(sub_head == h).astype(bf16) for h in range(heads)]

    def prefix_row(gaps):
        wide = jnp.broadcast_to(gaps, (8, rows)).astype(bf16)
        return mm(wide, upper_bf)[0:1]

    def after_column(gaps):
        return mm(jnp.where(col_ids > row_ids, gaps, 0.0).astype(bf16), ones)

    def bias(delta):
        whole = jnp.maximum(delta, 0.0).astype(jnp.int32)
        bucket = jnp.minimum(32 - lax.clz(whole), buckets - 1)
        return jnp.concatenate(
            [jnp.take_along_axis(table, bucket, axis=1) for table in tables], axis=1
        )

    def by_head_rows(q):
        return jnp.concatenate([q * mask for mask in lane_masks], axis=0)

    def by_head_lanes(g):
        return jnp.concatenate([g * mask for mask in sub_masks], axis=1)

    def own_heads(wide):
        return jnp.concatenate(
            [
                wide[h * head_dim : (h + 1) * head_dim, h * rows : (h + 1) * rows]
                for h in range(heads)
            ],
            axis=0,
        )

    def activate(products, biases, mask):
        scores = products * scaling + biases
        sig = 0.5 * jnp.tanh(0.5 * scores) + 0.5
        weights = scores * sig
        slope = sig + weights * (1.0 - sig)
        return (weights * mask).astype(bf16), slope * mask

    for copy in own[2:]:
        copy.wait()
    lanes = lax.broadcasted_iota(jnp.int32, (rows, rows), 1)
    tables = []
    for h in range(heads):
        table = jnp.zeros((rows, rows), f32)
        for b in range(buckets):
            table = jnp.where(lanes == b, table_ref[h, b], table)
        tables.append(table)
    own_gaps = gaps_ref[...].astype(f32)
    own_total = jnp.sum(own_gaps, axis=1, keepdims=True)
    own_row = prefix_row(own_gaps)
    own_after = after_column(own_gaps)
    diag_bias = bias(own_row + own_after - own_total)
    diag_mask = jnp.concatenate([upper] * heads, axis=1)
    gain = gain_ref[...]
    gates = gate_ref[...].astype(f32)
    upstream = cot_ref[...].astype(f32)
    scaled = (upstream * gates * gain).T

    keys = kbuf[0]
    values = vbuf[0]
    queries = by_head_rows(qbuf[0])
    diag_weights, diag_slope = activate(mm_nt(keys, queries), diag_bias, diag_mask)
    attended = mm(values.T, diag_weights)

    for k in range(1, reach + 1):
        to_earlier(k, lambda k=k: gaps_up(k).wait_recv())
        to_later(k, lambda k=k: gaps_down(k).wait_recv())

    def between(buf, d):
        if d == 1:
            return jnp.zeros((1, 1), f32)
        return jnp.sum(
            jnp.sum(buf[0 : d - 1].astype(f32), axis=0), axis=1, keepdims=True
        )

    biases = []
    for s, d in enumerate(offsets):
        after = after_column(gprev[d - 1].astype(f32))
        biases.append(bias(own_row + after + between(gprev, d)))
    def receive(s):
        for which in range(2):

            def arrived(which=which):
                wait_block(which, s)
                relay_up(which, s)

            to_earlier(offsets[s], arrived)

    for s in [s for s in (1, 0) if s < count] + list(range(2, count)):
        receive(s)
    early_keys = kbuf[1 : count + 1].reshape(count * rows, feats)
    early_values = vbuf[1 : count + 1].reshape(count * rows, feats)
    early_scores = mm_nt(early_keys, queries)
    early_weights = []
    for s in range(count):
        listed = (lists_ref[me, s] >= 0).astype(f32)
        part = early_scores[s * rows : (s + 1) * rows]
        weights, slope = activate(part, biases[s], listed)
        slope_q[s] = slope
        early_weights.append(weights)
    attended = attended + mm(early_values.T, jnp.concatenate(early_weights, axis=0))

    flat = own_heads(attended)
    own_sums = [
        jnp.sum(x, axis=0, keepdims=True) for x in (flat, flat * flat, scaled, scaled * flat)
    ]
    sums_out[...] = jnp.concatenate(own_sums + [jnp.zeros((4, rows), f32)], axis=0)
    for r in range(1, head_devices):
        sums_to(r).start()

    for s, d in enumerate(offsets):
        to_later(d, lambda s=s: queries_down(s).wait_recv())
    late_queries = jnp.concatenate([by_head_rows(qbuf[s + 1]) for s in range(count)], axis=0)
    late_scores = mm_nt(keys, late_queries)
    wide = heads * rows
    for s, d in enumerate(offsets):
        row = prefix_row(glater[d - 1].astype(f32))
        later_bias = bias(row + own_after + between(glater, d))
        there = jnp.minimum(me + d, groups - 1)
        listed = ((lists_ref[there, s] >= 0) & (me + d < groups)).astype(f32)
        part = late_scores[:, s * wide : (s + 1) * wide]
        weights, slope = activate(part, later_bias, listed)
        weight_k[:, s * wide : (s + 1) * wide] = weights
        slope_k[:, s * wide : (s + 1) * wide] = slope

    for r in range(1, head_devices):
        sums_to(r).wait_recv()
    sums = sums_out[...]
    for r in range(1, head_devices):
        sums = sums + sums_in[r - 1]
    mean = sums[0:1] / full_width
    var = sums[1:2] / full_width - mean * mean
    inv_std = lax.rsqrt(var + norm_eps)
    centered = (flat - mean) * inv_std
    scaled_mean = sums[2:3] / full_width
    product_mean = inv_std * (sums[3:4] - mean * sums[2:3]) / full_width
    grad = (inv_std * (scaled - scaled_mean - centered * product_mean)).astype(bf16)
    gabuf[0] = grad
    for s in range(count):
        to_earlier(offsets[s], lambda s=s: grads_down(s).start())

    grads = by_head_lanes(grad)
    diag_grad = (mm(values, grads) * diag_slope).astype(bf16)
    early_products = mm(early_values, grads)
    grad_scores = jnp.concatenate(
        [
            (early_products[s * rows : (s + 1) * rows] * slope_q[s]).astype(bf16)
            for s in range(count)
        ],
        axis=0,
    )
    dq = mm(keys.T, diag_grad) + mm(early_keys.T, grad_scores)
    dk = mm(diag_grad, queries)
    dv = mm_nt(diag_weights, grads)
    dq_ref[...] = (own_heads(dq) * scaling).T.astype(bf16)
    normed = centered.T * gain
    layer_ref[...] = (normed * gates).astype(bf16)
    dgate_ref[...] = (upstream * normed).astype(bf16)

    for s, d in enumerate(offsets):
        to_later(d, lambda s=s: grads_down(s).wait_recv())
    late_grads = jnp.concatenate([by_head_lanes(gabuf[s + 1]) for s in range(count)], axis=1)
    late_products = (mm(values, late_grads) * slope_k[...]).astype(bf16)
    dk = dk + mm(late_products, late_queries)
    dv = dv + mm_nt(weight_k[...], late_grads)
    dk_ref[...] = (dk * scaling).astype(bf16)
    dv_ref[...] = dv.astype(bf16)

    for k in range(1, reach + 1):
        to_later(k, lambda k=k: gaps_up(k).wait_send())
        to_earlier(k, lambda k=k: gaps_down(k).wait_send())
    for s, d in enumerate(offsets):
        if s == 0:
            sent_up = ((me % 2 == 0) & (me + 1 < groups)) | ((me % 2 == 1) & (me >= 2))
        elif s == 1:
            sent_up = me + 2 < groups
        else:
            sent_up = (me >= d // 2) & (me + d // 2 < groups)
        for which in range(2):
            pl.when(sent_up)(lambda which=which, s=s: wait_block_sent(which, s))
        to_earlier(d, lambda s=s: queries_down(s).wait_send())
        to_earlier(d, lambda s=s: grads_down(s).wait_send())
    for r in range(1, head_devices):
        sums_to(r).wait_send()


def hand_out(*refs):
    sems = refs[-1]
    copies = [pltpu.make_async_copy(refs[i], refs[i + 5], sems.at[i]) for i in range(5)]
    for copy in copies:
        copy.start()
    for copy in copies:
        copy.wait()


def per_device(
    query_rows,
    key_rows,
    value_rows,
    gate_rows,
    cotangent,
    event_gaps,
    block_lists,
    bias_table,
    norm_gain,
):
    rows, feats = query_rows.shape
    heads = bias_table.shape[0]
    groups = lax.axis_size("seq")
    head_devices = lax.axis_size("head")
    offsets = [2**s for s in range(block_lists.shape[1]) if 2**s < groups]
    count = len(offsets)
    reach = offsets[-1]
    hbm = pl.BlockSpec(memory_space=pltpu.HBM)
    vmem = pl.BlockSpec(memory_space=pltpu.VMEM)
    dma = pltpu.SemaphoreType.DMA
    operands = (
        query_rows,
        key_rows,
        value_rows,
        gate_rows,
        cotangent,
        event_gaps.reshape(1, rows),
        block_lists,
        bias_table,
        norm_gain.reshape(1, feats),
    )
    results = pl.pallas_call(
        functools.partial(kernel, groups, head_devices, offsets),
        out_shape=[pltpu.VMEM((rows, feats), bf16)] * 5,
        in_specs=[hbm] * 9,
        out_specs=[vmem] * 5,
        scratch_shapes=[
            pltpu.VMEM((rows, feats), bf16),
            pltpu.VMEM((rows, feats), bf16),
            pltpu.VMEM((1, rows), jnp.int32),
            pltpu.VMEM((1, feats), f32),
            pltpu.SMEM(block_lists.shape, jnp.int32),
            pltpu.SMEM(bias_table.shape, f32),
            pltpu.VMEM((count + 1, rows, feats), bf16),
            pltpu.VMEM((count + 1, rows, feats), bf16),
            pltpu.VMEM((count + 1, rows, feats), bf16),
            pltpu.VMEM((count + 1, feats, rows), bf16),
            pltpu.VMEM((reach, 1, rows), jnp.int32),
            pltpu.VMEM((reach, 1, rows), jnp.int32),
            pltpu.VMEM((8, rows), f32),
            pltpu.VMEM((head_devices - 1, 8, rows), f32),
            pltpu.VMEM((count, rows, heads * rows), f32),
            pltpu.VMEM((rows, count * heads * rows), f32),
            pltpu.VMEM((rows, count * heads * rows), bf16),
            dma((9,)),
            dma((2, reach)),
            dma((2, reach)),
            dma((count,)),
            dma((count,)),
            dma((2, count)),
            dma((2, count)),
            dma((head_devices - 1,)),
            dma((head_devices - 1,)),
            dma((count,)),
            dma((count,)),
        ],
        compiler_params=pltpu.CompilerParams(
            collective_id=0, has_side_effects=True, vmem_limit_bytes=24 * 2**20
        ),
    )(*[pltpu.with_memory_space_constraint(x, pltpu.HBM) for x in operands])
    return pl.pallas_call(
        hand_out,
        out_shape=[jax.ShapeDtypeStruct((rows, feats), bf16)] * 5,
        in_specs=[vmem] * 5,
        out_specs=[hbm] * 5,
        scratch_shapes=[dma((5,))],
        compiler_params=pltpu.CompilerParams(vmem_limit_bytes=2**20),
    )(*[pltpu.with_memory_space_constraint(x, pltpu.VMEM) for x in results])


def solution(mesh):
    placed = P("seq", "head")
    return jax.shard_map(
        per_device,
        mesh=mesh,
        in_specs=(
            placed,
            placed,
            placed,
            placed,
            placed,
            P("seq"),
            P(),
            P("head", None),
            P("head"),
        ),
        out_specs=(placed,) * 5,
        check_vma=False,
    )
```

```python
import functools

import jax
import jax.numpy as jnp
from jax import lax
from jax.experimental import pallas as pl
from jax.experimental.pallas import tpu as pltpu
from jax.sharding import PartitionSpec as P

norm_eps = 1e-05
f32 = jnp.float32
bf16 = jnp.bfloat16
MESH = pl.DeviceIdType.MESH


def mm(a, b):
    return lax.dot_general(a, b, (((1,), (0,)), ((), ())), preferred_element_type=f32)


def mm_nt(a, b):
    return lax.dot_general(a, b, (((1,), (1,)), ((), ())), preferred_element_type=f32)


def kernel(
    groups,
    head_devices,
    offsets,
    q_in,
    k_in,
    v_in,
    gate_in,
    cot_in,
    gaps_in,
    lists_in,
    table_in,
    gain_in,
    layer_ref,
    dq_ref,
    dk_ref,
    dv_ref,
    dgate_ref,
    gate_ref,
    cot_ref,
    gaps_ref,
    gain_ref,
    lists_ref,
    table_ref,
    qbuf,
    kbuf,
    vbuf,
    gabuf,
    gprev,
    glater,
    sums_out,
    sums_in,
    slope_q,
    slope_k,
    weight_k,
    local_sem,
    gap_send,
    gap_recv,
    q_send,
    q_recv,
    kv_send,
    kv_recv,
    sum_send,
    sum_recv,
    ga_send,
    ga_recv,
):
    rows, feats = q_in.shape
    heads, buckets = table_in.shape
    head_dim = feats // heads
    scaling = head_dim**-0.5
    full_width = feats * head_devices
    reach = offsets[-1]
    count = len(offsets)
    me = lax.axis_index("seq")
    head = lax.axis_index("head")

    def to_later(d, body):
        pl.when(me + d < groups)(body)

    def to_earlier(d, body):
        pl.when(me >= d)(body)

    pairs = (
        (gaps_in, gaps_ref),
        (table_in, table_ref),
        (lists_in, lists_ref),
        (gain_in, gain_ref),
        (k_in, kbuf.at[0]),
        (q_in, qbuf.at[0]),
        (v_in, vbuf.at[0]),
        (gate_in, gate_ref),
        (cot_in, cot_ref),
    )
    own = [pltpu.make_async_copy(src, dst, local_sem.at[i]) for i, (src, dst) in enumerate(pairs)]
    for copy in own:
        copy.start()

    barrier = pltpu.get_barrier_semaphore()

    def greet(axis, where):
        pl.semaphore_signal(barrier, inc=1, device_id={axis: where}, device_id_type=MESH)

    for k in range(1, reach + 1):
        to_later(k, lambda k=k: greet("seq", me + k))
        to_earlier(k, lambda k=k: greet("seq", me - k))
    for r in range(1, head_devices):
        greet("head", lax.rem(head + r, head_devices))
    pl.semaphore_wait(
        barrier,
        jnp.minimum(me, reach) + jnp.minimum(groups - 1 - me, reach) + head_devices - 1,
    )

    def remote(src, dst, send, recv, axis, where):
        return pltpu.make_async_remote_copy(
            src_ref=src,
            dst_ref=dst,
            send_sem=send,
            recv_sem=recv,
            device_id={axis: where},
            device_id_type=MESH,
        )

    def gaps_up(k):
        return remote(
            gaps_in, gprev.at[k - 1], gap_send.at[0, k - 1], gap_recv.at[0, k - 1], "seq", me + k
        )

    def gaps_down(k):
        return remote(
            gaps_in, glater.at[k - 1], gap_send.at[1, k - 1], gap_recv.at[1, k - 1], "seq", me - k
        )

    def keys_up(s):
        return remote(
            k_in, kbuf.at[s + 1], kv_send.at[0, s], kv_recv.at[0, s], "seq", me + offsets[s]
        )

    def values_up(s):
        return remote(
            v_in, vbuf.at[s + 1], kv_send.at[1, s], kv_recv.at[1, s], "seq", me + offsets[s]
        )

    def queries_down(s):
        return remote(q_in, qbuf.at[s + 1], q_send.at[s], q_recv.at[s], "seq", me - offsets[s])

    def grads_down(s):
        return remote(
            gabuf.at[0], gabuf.at[s + 1], ga_send.at[s], ga_recv.at[s], "seq", me - offsets[s]
        )

    def sums_to(r):
        return remote(
            sums_out,
            sums_in.at[r - 1],
            sum_send.at[r - 1],
            sum_recv.at[r - 1],
            "head",
            lax.rem(head + r, head_devices),
        )

    for k in range(1, reach + 1):
        to_later(k, lambda k=k: gaps_up(k).start())
        to_earlier(k, lambda k=k: gaps_down(k).start())
    for s in reversed(range(count)):
        to_later(offsets[s], lambda s=s: keys_up(s).start())
        to_later(offsets[s], lambda s=s: values_up(s).start())
    for s in reversed(range(count)):
        to_earlier(offsets[s], lambda s=s: queries_down(s).start())

    for k in range(1, reach + 1):

        def no_earlier(k=k):
            gprev[k - 1] = jnp.zeros_like(gprev[k - 1])

        def no_later(k=k):
            glater[k - 1] = jnp.zeros_like(glater[k - 1])

        pl.when(me < k)(no_earlier)
        pl.when(me + k >= groups)(no_later)
    for s, d in enumerate(offsets):

        def no_keys(s=s):
            kbuf[s + 1] = jnp.zeros((rows, feats), bf16)
            vbuf[s + 1] = jnp.zeros((rows, feats), bf16)

        def no_queries(s=s):
            qbuf[s + 1] = jnp.zeros((rows, feats), bf16)
            gabuf[s + 1] = jnp.zeros((feats, rows), bf16)

        pl.when(me < d)(no_keys)
        pl.when(me + d >= groups)(no_queries)

    row_ids = lax.broadcasted_iota(jnp.int32, (rows, rows), 0)
    col_ids = lax.broadcasted_iota(jnp.int32, (rows, rows), 1)
    upper = (row_ids <= col_ids).astype(f32)
    upper_bf = upper.astype(bf16)
    ones = jnp.ones((rows, rows), bf16)
    lane_head = lax.broadcasted_iota(jnp.int32, (rows, feats), 1) // head_dim
    sub_head = lax.broadcasted_iota(jnp.int32, (feats, rows), 0) // head_dim
    lane_masks = [(lane_head == h).astype(bf16) for h in range(heads)]
    sub_masks = [(sub_head == h).astype(bf16) for h in range(heads)]

    def prefix_row(gaps):
        wide = jnp.broadcast_to(gaps, (8, rows)).astype(bf16)
        return mm(wide, upper_bf)[0:1]

    def after_column(gaps):
        return mm(jnp.where(col_ids > row_ids, gaps, 0.0).astype(bf16), ones)

    def bias(delta):
        whole = jnp.maximum(delta, 0.0).astype(jnp.int32)
        bucket = jnp.minimum(32 - lax.clz(whole), buckets - 1)
        return jnp.concatenate(
            [jnp.take_along_axis(table, bucket, axis=1) for table in tables], axis=1
        )

    def by_head_rows(q):
        return jnp.concatenate([q * mask for mask in lane_masks], axis=0)

    def by_head_lanes(g):
        return jnp.concatenate([g * mask for mask in sub_masks], axis=1)

    def own_heads(wide):
        return jnp.concatenate(
            [
                wide[h * head_dim : (h + 1) * head_dim, h * rows : (h + 1) * rows]
                for h in range(heads)
            ],
            axis=0,
        )

    def activate(products, biases, mask):
        scores = products * scaling + biases
        sig = 0.5 * jnp.tanh(0.5 * scores) + 0.5
        weights = scores * sig
        slope = sig + weights * (1.0 - sig)
        return (weights * mask).astype(bf16), slope * mask

    for copy in own:
        copy.wait()
    lanes = lax.broadcasted_iota(jnp.int32, (rows, rows), 1)
    tables = []
    for h in range(heads):
        table = jnp.zeros((rows, rows), f32)
        for b in range(buckets):
            table = jnp.where(lanes == b, table_ref[h, b], table)
        tables.append(table)
    own_gaps = gaps_ref[...].astype(f32)
    own_total = jnp.sum(own_gaps, axis=1, keepdims=True)
    own_row = prefix_row(own_gaps)
    own_after = after_column(own_gaps)
    diag_bias = bias(own_row + own_after - own_total)
    diag_mask = jnp.concatenate([upper] * heads, axis=1)
    gain = gain_ref[...]
    gates = gate_ref[...].astype(f32)
    upstream = cot_ref[...].astype(f32)
    scaled = (upstream * gates * gain).T

    keys = kbuf[0]
    values = vbuf[0]
    queries = by_head_rows(qbuf[0])
    diag_weights, diag_slope = activate(mm_nt(keys, queries), diag_bias, diag_mask)
    attended = mm(values.T, diag_weights)

    for k in range(1, reach + 1):
        to_earlier(k, lambda k=k: gaps_up(k).wait_recv())
        to_later(k, lambda k=k: gaps_down(k).wait_recv())

    def between(buf, d):
        if d == 1:
            return jnp.zeros((1, 1), f32)
        return jnp.sum(
            jnp.sum(buf[0 : d - 1].astype(f32), axis=0), axis=1, keepdims=True
        )

    biases = []
    for s, d in enumerate(offsets):
        after = after_column(gprev[d - 1].astype(f32))
        biases.append(bias(own_row + after + between(gprev, d)))
    for s, d in enumerate(offsets):
        to_earlier(d, lambda s=s: keys_up(s).wait_recv())
        to_earlier(d, lambda s=s: values_up(s).wait_recv())
    early_keys = kbuf[1 : count + 1].reshape(count * rows, feats)
    early_values = vbuf[1 : count + 1].reshape(count * rows, feats)
    early_scores = mm_nt(early_keys, queries)
    early_weights = []
    for s in range(count):
        listed = (lists_ref[me, s] >= 0).astype(f32)
        part = early_scores[s * rows : (s + 1) * rows]
        weights, slope = activate(part, biases[s], listed)
        slope_q[s] = slope
        early_weights.append(weights)
    attended = attended + mm(early_values.T, jnp.concatenate(early_weights, axis=0))

    flat = own_heads(attended)
    own_sums = [
        jnp.sum(x, axis=0, keepdims=True) for x in (flat, flat * flat, scaled, scaled * flat)
    ]
    sums_out[...] = jnp.concatenate(own_sums + [jnp.zeros((4, rows), f32)], axis=0)
    for r in range(1, head_devices):
        sums_to(r).start()

    for s, d in enumerate(offsets):
        to_later(d, lambda s=s: queries_down(s).wait_recv())
    keys_t = keys.T
    early_keys_t = early_keys.T
    late_queries = jnp.concatenate([by_head_rows(qbuf[s + 1]) for s in range(count)], axis=0)
    late_scores = mm_nt(keys, late_queries)
    wide = heads * rows
    for s, d in enumerate(offsets):
        row = prefix_row(glater[d - 1].astype(f32))
        later_bias = bias(row + own_after + between(glater, d))
        there = jnp.minimum(me + d, groups - 1)
        listed = ((lists_ref[there, s] >= 0) & (me + d < groups)).astype(f32)
        part = late_scores[:, s * wide : (s + 1) * wide]
        weights, slope = activate(part, later_bias, listed)
        weight_k[:, s * wide : (s + 1) * wide] = weights
        slope_k[:, s * wide : (s + 1) * wide] = slope

    for r in range(1, head_devices):
        sums_to(r).wait_recv()
    sums = sums_out[...]
    for r in range(1, head_devices):
        sums = sums + sums_in[r - 1]
    mean = sums[0:1] / full_width
    var = sums[1:2] / full_width - mean * mean
    inv_std = lax.rsqrt(var + norm_eps)
    centered = (flat - mean) * inv_std
    scaled_mean = sums[2:3] / full_width
    product_mean = inv_std * (sums[3:4] - mean * sums[2:3]) / full_width
    grad = (inv_std * (scaled - scaled_mean - centered * product_mean)).astype(bf16)
    gabuf[0] = grad
    for s in reversed(range(count)):
        to_earlier(offsets[s], lambda s=s: grads_down(s).start())

    grads = by_head_lanes(grad)
    diag_grad = (mm(values, grads) * diag_slope).astype(bf16)
    early_products = mm(early_values, grads)
    grad_scores = jnp.concatenate(
        [
            (early_products[s * rows : (s + 1) * rows] * slope_q[s]).astype(bf16)
            for s in range(count)
        ],
        axis=0,
    )
    dq = mm(keys_t, diag_grad) + mm(early_keys_t, grad_scores)
    dk = mm(diag_grad, queries)
    dv = mm_nt(diag_weights, grads)
    dq_ref[...] = (own_heads(dq) * scaling).T.astype(bf16)
    normed = centered.T * gain
    layer_ref[...] = (normed * gates).astype(bf16)
    dgate_ref[...] = (upstream * normed).astype(bf16)

    for s, d in enumerate(offsets):
        to_later(d, lambda s=s: grads_down(s).wait_recv())
    late_grads = jnp.concatenate([by_head_lanes(gabuf[s + 1]) for s in range(count)], axis=1)
    late_products = (mm(values, late_grads) * slope_k[...]).astype(bf16)
    dk = dk + mm(late_products, late_queries)
    dv = dv + mm_nt(weight_k[...], late_grads)
    dk_ref[...] = (dk * scaling).astype(bf16)
    dv_ref[...] = dv.astype(bf16)

    for k in range(1, reach + 1):
        to_later(k, lambda k=k: gaps_up(k).wait_send())
        to_earlier(k, lambda k=k: gaps_down(k).wait_send())
    for s, d in enumerate(offsets):
        to_later(d, lambda s=s: keys_up(s).wait_send())
        to_later(d, lambda s=s: values_up(s).wait_send())
        to_earlier(d, lambda s=s: queries_down(s).wait_send())
        to_earlier(d, lambda s=s: grads_down(s).wait_send())
    for r in range(1, head_devices):
        sums_to(r).wait_send()


def hand_out(*refs):
    sems = refs[-1]
    copies = [pltpu.make_async_copy(refs[i], refs[i + 5], sems.at[i]) for i in range(5)]
    for copy in copies:
        copy.start()
    for copy in copies:
        copy.wait()


def per_device(
    query_rows,
    key_rows,
    value_rows,
    gate_rows,
    cotangent,
    event_gaps,
    block_lists,
    bias_table,
    norm_gain,
):
    rows, feats = query_rows.shape
    heads = bias_table.shape[0]
    groups = lax.axis_size("seq")
    head_devices = lax.axis_size("head")
    offsets = [2**s for s in range(block_lists.shape[1]) if 2**s < groups]
    count = len(offsets)
    reach = offsets[-1]
    hbm = pl.BlockSpec(memory_space=pltpu.HBM)
    vmem = pl.BlockSpec(memory_space=pltpu.VMEM)
    dma = pltpu.SemaphoreType.DMA
    operands = (
        query_rows,
        key_rows,
        value_rows,
        gate_rows,
        cotangent,
        event_gaps.reshape(1, rows),
        block_lists,
        bias_table,
        norm_gain.reshape(1, feats),
    )
    results = pl.pallas_call(
        functools.partial(kernel, groups, head_devices, offsets),
        out_shape=[pltpu.VMEM((rows, feats), bf16)] * 5,
        in_specs=[hbm] * 9,
        out_specs=[vmem] * 5,
        scratch_shapes=[
            pltpu.VMEM((rows, feats), bf16),
            pltpu.VMEM((rows, feats), bf16),
            pltpu.VMEM((1, rows), jnp.int32),
            pltpu.VMEM((1, feats), f32),
            pltpu.SMEM(block_lists.shape, jnp.int32),
            pltpu.SMEM(bias_table.shape, f32),
            pltpu.VMEM((count + 1, rows, feats), bf16),
            pltpu.VMEM((count + 1, rows, feats), bf16),
            pltpu.VMEM((count + 1, rows, feats), bf16),
            pltpu.VMEM((count + 1, feats, rows), bf16),
            pltpu.VMEM((reach, 1, rows), jnp.int32),
            pltpu.VMEM((reach, 1, rows), jnp.int32),
            pltpu.VMEM((8, rows), f32),
            pltpu.VMEM((head_devices - 1, 8, rows), f32),
            pltpu.VMEM((count, rows, heads * rows), f32),
            pltpu.VMEM((rows, count * heads * rows), f32),
            pltpu.VMEM((rows, count * heads * rows), bf16),
            dma((9,)),
            dma((2, reach)),
            dma((2, reach)),
            dma((count,)),
            dma((count,)),
            dma((2, count)),
            dma((2, count)),
            dma((head_devices - 1,)),
            dma((head_devices - 1,)),
            dma((count,)),
            dma((count,)),
        ],
        compiler_params=pltpu.CompilerParams(
            collective_id=0, has_side_effects=True, vmem_limit_bytes=24 * 2**20
        ),
    )(*[pltpu.with_memory_space_constraint(x, pltpu.HBM) for x in operands])
    return pl.pallas_call(
        hand_out,
        out_shape=[jax.ShapeDtypeStruct((rows, feats), bf16)] * 5,
        in_specs=[vmem] * 5,
        out_specs=[hbm] * 5,
        scratch_shapes=[dma((5,))],
        compiler_params=pltpu.CompilerParams(vmem_limit_bytes=2**20),
    )(*[pltpu.with_memory_space_constraint(x, pltpu.VMEM) for x in results])


def solution(mesh):
    placed = P("seq", "head")
    return jax.shard_map(
        per_device,
        mesh=mesh,
        in_specs=(
            placed,
            placed,
            placed,
            placed,
            placed,
            P("seq"),
            P(),
            P("head", None),
            P("head"),
        ),
        out_specs=(placed,) * 5,
        check_vma=False,
    )
```

```python
import functools

import jax
import jax.numpy as jnp
from jax import lax
from jax.experimental import pallas as pl
from jax.experimental.pallas import tpu as pltpu
from jax.sharding import PartitionSpec as P

norm_eps = 1e-05
f32 = jnp.float32
bf16 = jnp.bfloat16
MESH = pl.DeviceIdType.MESH


def mm(a, b):
    return lax.dot_general(a, b, (((1,), (0,)), ((), ())), preferred_element_type=f32)


def mm_nt(a, b):
    return lax.dot_general(a, b, (((1,), (1,)), ((), ())), preferred_element_type=f32)


def kernel(
    groups,
    head_devices,
    offsets,
    q_in,
    k_in,
    v_in,
    gate_in,
    cot_in,
    gaps_in,
    lists_in,
    table_in,
    gain_in,
    layer_ref,
    dq_ref,
    dk_ref,
    dv_ref,
    dgate_ref,
    gate_ref,
    cot_ref,
    gaps_ref,
    gain_ref,
    lists_ref,
    table_ref,
    qbuf,
    kbuf,
    vbuf,
    gabuf,
    gprev,
    glater,
    sums_out,
    sums_in,
    slope_q,
    slope_k,
    weight_k,
    local_sem,
    gap_send,
    gap_recv,
    q_send,
    q_recv,
    kv_send,
    kv_recv,
    sum_send,
    sum_recv,
    ga_send,
    ga_recv,
):
    rows, feats = q_in.shape
    heads, buckets = table_in.shape
    head_dim = feats // heads
    scaling = head_dim**-0.5
    full_width = feats * head_devices
    reach = offsets[-1]
    count = len(offsets)
    me = lax.axis_index("seq")
    head = lax.axis_index("head")

    def to_later(d, body):
        pl.when(me + d < groups)(body)

    def to_earlier(d, body):
        pl.when(me >= d)(body)

    pairs = (
        (gaps_in, gaps_ref),
        (table_in, table_ref),
        (lists_in, lists_ref),
        (gain_in, gain_ref),
        (k_in, kbuf.at[0]),
        (q_in, qbuf.at[0]),
        (v_in, vbuf.at[0]),
        (gate_in, gate_ref),
        (cot_in, cot_ref),
    )
    own = [pltpu.make_async_copy(src, dst, local_sem.at[i]) for i, (src, dst) in enumerate(pairs)]
    for copy in own:
        copy.start()

    barrier = pltpu.get_barrier_semaphore()

    def greet(axis, where):
        pl.semaphore_signal(barrier, inc=1, device_id={axis: where}, device_id_type=MESH)

    for k in range(1, reach + 1):
        to_later(k, lambda k=k: greet("seq", me + k))
        to_earlier(k, lambda k=k: greet("seq", me - k))
    for r in range(1, head_devices):
        greet("head", lax.rem(head + r, head_devices))
    pl.semaphore_wait(
        barrier,
        jnp.minimum(me, reach) + jnp.minimum(groups - 1 - me, reach) + head_devices - 1,
    )

    def remote(src, dst, send, recv, axis, where):
        return pltpu.make_async_remote_copy(
            src_ref=src,
            dst_ref=dst,
            send_sem=send,
            recv_sem=recv,
            device_id={axis: where},
            device_id_type=MESH,
        )

    def gaps_up(k):
        return remote(
            gaps_in, gprev.at[k - 1], gap_send.at[0, k - 1], gap_recv.at[0, k - 1], "seq", me + k
        )

    def gaps_down(k):
        return remote(
            gaps_in, glater.at[k - 1], gap_send.at[1, k - 1], gap_recv.at[1, k - 1], "seq", me - k
        )

    def keys_up(s):
        return remote(
            k_in, kbuf.at[s + 1], kv_send.at[0, s], kv_recv.at[0, s], "seq", me + offsets[s]
        )

    def values_up(s):
        return remote(
            v_in, vbuf.at[s + 1], kv_send.at[1, s], kv_recv.at[1, s], "seq", me + offsets[s]
        )

    def queries_down(s):
        return remote(q_in, qbuf.at[s + 1], q_send.at[s], q_recv.at[s], "seq", me - offsets[s])

    def grads_down(s):
        return remote(
            gabuf.at[0], gabuf.at[s + 1], ga_send.at[s], ga_recv.at[s], "seq", me - offsets[s]
        )

    def sums_to(r):
        return remote(
            sums_out,
            sums_in.at[r - 1],
            sum_send.at[r - 1],
            sum_recv.at[r - 1],
            "head",
            lax.rem(head + r, head_devices),
        )

    for k in range(1, reach + 1):
        to_later(k, lambda k=k: gaps_up(k).start())
        to_earlier(k, lambda k=k: gaps_down(k).start())
    for s in range(count):
        to_later(offsets[s], lambda s=s: keys_up(s).start())
        to_later(offsets[s], lambda s=s: values_up(s).start())
        to_earlier(offsets[s], lambda s=s: queries_down(s).start())

    for k in range(1, reach + 1):

        def no_earlier(k=k):
            gprev[k - 1] = jnp.zeros_like(gprev[k - 1])

        def no_later(k=k):
            glater[k - 1] = jnp.zeros_like(glater[k - 1])

        pl.when(me < k)(no_earlier)
        pl.when(me + k >= groups)(no_later)
    for s, d in enumerate(offsets):

        def no_keys(s=s):
            kbuf[s + 1] = jnp.zeros((rows, feats), bf16)
            vbuf[s + 1] = jnp.zeros((rows, feats), bf16)

        def no_queries(s=s):
            qbuf[s + 1] = jnp.zeros((rows, feats), bf16)
            gabuf[s + 1] = jnp.zeros((feats, rows), bf16)

        pl.when(me < d)(no_keys)
        pl.when(me + d >= groups)(no_queries)

    row_ids = lax.broadcasted_iota(jnp.int32, (rows, rows), 0)
    col_ids = lax.broadcasted_iota(jnp.int32, (rows, rows), 1)
    upper = (row_ids <= col_ids).astype(f32)
    upper_bf = upper.astype(bf16)
    ones = jnp.ones((rows, rows), bf16)
    lane_head = lax.broadcasted_iota(jnp.int32, (rows, feats), 1) // head_dim
    sub_head = lax.broadcasted_iota(jnp.int32, (feats, rows), 0) // head_dim
    lane_masks = [(lane_head == h).astype(bf16) for h in range(heads)]
    sub_masks = [(sub_head == h).astype(bf16) for h in range(heads)]

    def prefix_row(gaps):
        wide = jnp.broadcast_to(gaps, (8, rows)).astype(bf16)
        return mm(wide, upper_bf)[0:1]

    def after_column(gaps):
        return mm(jnp.where(col_ids > row_ids, gaps, 0.0).astype(bf16), ones)

    def bias(delta):
        whole = jnp.maximum(delta, 0.0).astype(jnp.int32)
        bucket = jnp.minimum(32 - lax.clz(whole), buckets - 1)
        return jnp.concatenate(
            [jnp.take_along_axis(table, bucket, axis=1) for table in tables], axis=1
        )

    def by_head_rows(q):
        return jnp.concatenate([q * mask for mask in lane_masks], axis=0)

    def by_head_lanes(g):
        return jnp.concatenate([g * mask for mask in sub_masks], axis=1)

    def own_heads(wide):
        return jnp.concatenate(
            [
                wide[h * head_dim : (h + 1) * head_dim, h * rows : (h + 1) * rows]
                for h in range(heads)
            ],
            axis=0,
        )

    def activate(products, biases, mask):
        scores = products * scaling + biases
        sig = 0.5 * jnp.tanh(0.5 * scores) + 0.5
        weights = scores * sig
        slope = sig + weights * (1.0 - sig)
        return (weights * mask).astype(bf16), slope * mask

    for copy in own:
        copy.wait()
    lanes = lax.broadcasted_iota(jnp.int32, (rows, rows), 1)
    tables = []
    for h in range(heads):
        table = jnp.zeros((rows, rows), f32)
        for b in range(buckets):
            table = jnp.where(lanes == b, table_ref[h, b], table)
        tables.append(table)
    own_gaps = gaps_ref[...].astype(f32)
    own_total = jnp.sum(own_gaps, axis=1, keepdims=True)
    own_row = prefix_row(own_gaps)
    own_after = after_column(own_gaps)
    diag_bias = bias(own_row + own_after - own_total)
    diag_mask = jnp.concatenate([upper] * heads, axis=1)
    gain = gain_ref[...]
    gates = gate_ref[...].astype(f32)
    upstream = cot_ref[...].astype(f32)
    scaled = (upstream * gates * gain).T

    keys = kbuf[0]
    values = vbuf[0]
    queries = by_head_rows(qbuf[0])
    diag_weights, diag_slope = activate(mm_nt(keys, queries), diag_bias, diag_mask)
    attended = mm(values.T, diag_weights)

    for k in range(1, reach + 1):
        to_earlier(k, lambda k=k: gaps_up(k).wait_recv())
        to_later(k, lambda k=k: gaps_down(k).wait_recv())

    def between(buf, d):
        if d == 1:
            return jnp.zeros((1, 1), f32)
        return jnp.sum(
            jnp.sum(buf[0 : d - 1].astype(f32), axis=0), axis=1, keepdims=True
        )

    biases = []
    for s, d in enumerate(offsets):
        after = after_column(gprev[d - 1].astype(f32))
        biases.append(bias(own_row + after + between(gprev, d)))
    for s, d in enumerate(offsets):
        to_earlier(d, lambda s=s: keys_up(s).wait_recv())
        to_earlier(d, lambda s=s: values_up(s).wait_recv())
    early_keys = kbuf[1 : count + 1].reshape(count * rows, feats)
    early_values = vbuf[1 : count + 1].reshape(count * rows, feats)
    early_scores = mm_nt(early_keys, queries)
    early_weights = []
    for s in range(count):
        listed = (lists_ref[me, s] >= 0).astype(f32)
        part = early_scores[s * rows : (s + 1) * rows]
        weights, slope = activate(part, biases[s], listed)
        slope_q[s] = slope
        early_weights.append(weights)
    attended = attended + mm(early_values.T, jnp.concatenate(early_weights, axis=0))

    flat = own_heads(attended)
    own_sums = [
        jnp.sum(x, axis=0, keepdims=True) for x in (flat, flat * flat, scaled, scaled * flat)
    ]
    sums_out[...] = jnp.concatenate(own_sums + [jnp.zeros((4, rows), f32)], axis=0)
    for r in range(1, head_devices):
        sums_to(r).start()

    for s, d in enumerate(offsets):
        to_later(d, lambda s=s: queries_down(s).wait_recv())
    keys_t = keys.T
    early_keys_t = early_keys.T
    late_queries = jnp.concatenate([by_head_rows(qbuf[s + 1]) for s in range(count)], axis=0)
    late_scores = mm_nt(keys, late_queries)
    wide = heads * rows
    for s, d in enumerate(offsets):
        row = prefix_row(glater[d - 1].astype(f32))
        later_bias = bias(row + own_after + between(glater, d))
        there = jnp.minimum(me + d, groups - 1)
        listed = ((lists_ref[there, s] >= 0) & (me + d < groups)).astype(f32)
        part = late_scores[:, s * wide : (s + 1) * wide]
        weights, slope = activate(part, later_bias, listed)
        weight_k[:, s * wide : (s + 1) * wide] = weights
        slope_k[:, s * wide : (s + 1) * wide] = slope

    for r in range(1, head_devices):
        sums_to(r).wait_recv()
    sums = sums_out[...]
    for r in range(1, head_devices):
        sums = sums + sums_in[r - 1]
    mean = sums[0:1] / full_width
    var = sums[1:2] / full_width - mean * mean
    inv_std = lax.rsqrt(var + norm_eps)
    centered = (flat - mean) * inv_std
    scaled_mean = sums[2:3] / full_width
    product_mean = inv_std * (sums[3:4] - mean * sums[2:3]) / full_width
    grad = (inv_std * (scaled - scaled_mean - centered * product_mean)).astype(bf16)
    gabuf[0] = grad
    for s in reversed(range(count)):
        to_earlier(offsets[s], lambda s=s: grads_down(s).start())

    grads = by_head_lanes(grad)
    diag_grad = (mm(values, grads) * diag_slope).astype(bf16)
    early_products = mm(early_values, grads)
    grad_scores = jnp.concatenate(
        [
            (early_products[s * rows : (s + 1) * rows] * slope_q[s]).astype(bf16)
            for s in range(count)
        ],
        axis=0,
    )
    dq = mm(keys_t, diag_grad) + mm(early_keys_t, grad_scores)
    dk = mm(diag_grad, queries)
    dv = mm_nt(diag_weights, grads)
    dq_ref[...] = (own_heads(dq) * scaling).T.astype(bf16)
    normed = centered.T * gain
    layer_ref[...] = (normed * gates).astype(bf16)
    dgate_ref[...] = (upstream * normed).astype(bf16)

    for s, d in enumerate(offsets):
        to_later(d, lambda s=s: grads_down(s).wait_recv())
    late_grads = jnp.concatenate([by_head_lanes(gabuf[s + 1]) for s in range(count)], axis=1)
    late_products = (mm(values, late_grads) * slope_k[...]).astype(bf16)
    dk = dk + mm(late_products, late_queries)
    dv = dv + mm_nt(weight_k[...], late_grads)
    dk_ref[...] = (dk * scaling).astype(bf16)
    dv_ref[...] = dv.astype(bf16)

    for k in range(1, reach + 1):
        to_later(k, lambda k=k: gaps_up(k).wait_send())
        to_earlier(k, lambda k=k: gaps_down(k).wait_send())
    for s, d in enumerate(offsets):
        to_later(d, lambda s=s: keys_up(s).wait_send())
        to_later(d, lambda s=s: values_up(s).wait_send())
        to_earlier(d, lambda s=s: queries_down(s).wait_send())
        to_earlier(d, lambda s=s: grads_down(s).wait_send())
    for r in range(1, head_devices):
        sums_to(r).wait_send()


def hand_out(*refs):
    sems = refs[-1]
    copies = [pltpu.make_async_copy(refs[i], refs[i + 5], sems.at[i]) for i in range(5)]
    for copy in copies:
        copy.start()
    for copy in copies:
        copy.wait()


def per_device(
    query_rows,
    key_rows,
    value_rows,
    gate_rows,
    cotangent,
    event_gaps,
    block_lists,
    bias_table,
    norm_gain,
):
    rows, feats = query_rows.shape
    heads = bias_table.shape[0]
    groups = lax.axis_size("seq")
    head_devices = lax.axis_size("head")
    offsets = [2**s for s in range(block_lists.shape[1]) if 2**s < groups]
    count = len(offsets)
    reach = offsets[-1]
    hbm = pl.BlockSpec(memory_space=pltpu.HBM)
    vmem = pl.BlockSpec(memory_space=pltpu.VMEM)
    dma = pltpu.SemaphoreType.DMA
    operands = (
        query_rows,
        key_rows,
        value_rows,
        gate_rows,
        cotangent,
        event_gaps.reshape(1, rows),
        block_lists,
        bias_table,
        norm_gain.reshape(1, feats),
    )
    results = pl.pallas_call(
        functools.partial(kernel, groups, head_devices, offsets),
        out_shape=[pltpu.VMEM((rows, feats), bf16)] * 5,
        in_specs=[hbm] * 9,
        out_specs=[vmem] * 5,
        scratch_shapes=[
            pltpu.VMEM((rows, feats), bf16),
            pltpu.VMEM((rows, feats), bf16),
            pltpu.VMEM((1, rows), jnp.int32),
            pltpu.VMEM((1, feats), f32),
            pltpu.SMEM(block_lists.shape, jnp.int32),
            pltpu.SMEM(bias_table.shape, f32),
            pltpu.VMEM((count + 1, rows, feats), bf16),
            pltpu.VMEM((count + 1, rows, feats), bf16),
            pltpu.VMEM((count + 1, rows, feats), bf16),
            pltpu.VMEM((count + 1, feats, rows), bf16),
            pltpu.VMEM((reach, 1, rows), jnp.int32),
            pltpu.VMEM((reach, 1, rows), jnp.int32),
            pltpu.VMEM((8, rows), f32),
            pltpu.VMEM((head_devices - 1, 8, rows), f32),
            pltpu.VMEM((count, rows, heads * rows), f32),
            pltpu.VMEM((rows, count * heads * rows), f32),
            pltpu.VMEM((rows, count * heads * rows), bf16),
            dma((9,)),
            dma((2, reach)),
            dma((2, reach)),
            dma((count,)),
            dma((count,)),
            dma((2, count)),
            dma((2, count)),
            dma((head_devices - 1,)),
            dma((head_devices - 1,)),
            dma((count,)),
            dma((count,)),
        ],
        compiler_params=pltpu.CompilerParams(
            collective_id=0, has_side_effects=True, vmem_limit_bytes=24 * 2**20
        ),
    )(*[pltpu.with_memory_space_constraint(x, pltpu.HBM) for x in operands])
    return pl.pallas_call(
        hand_out,
        out_shape=[jax.ShapeDtypeStruct((rows, feats), bf16)] * 5,
        in_specs=[vmem] * 5,
        out_specs=[hbm] * 5,
        scratch_shapes=[dma((5,))],
        compiler_params=pltpu.CompilerParams(vmem_limit_bytes=2**20),
    )(*[pltpu.with_memory_space_constraint(x, pltpu.VMEM) for x in results])


def solution(mesh):
    placed = P("seq", "head")
    return jax.shard_map(
        per_device,
        mesh=mesh,
        in_specs=(
            placed,
            placed,
            placed,
            placed,
            placed,
            P("seq"),
            P(),
            P("head", None),
            P("head"),
        ),
        out_specs=(placed,) * 5,
        check_vma=False,
    )
```
